256 devices in a mesh: ta: 4 (over x_lo, core), gz: 4 (over y), gy: 16 (over z, x_hi).
Axes of the slice: x: 4 (x_hi: 2, x_lo: 2; x = x_hi * 2 + x_lo), y: 4, z: 8, core: 2. Of those that a mesh axis runs over, the one named last changes fastest.
Arguments:
- eigenvectors: bfloat16 [2, 3, 96, 294912], P(None, None, None, ('ta', 'gz', 'gy')), parts along dimension 3, may hold values from -0.015625 to 0.015625
- gauge_links: bfloat16 [2, 3, 3, 3, 294912], P(None, None, None, None, ('ta', 'gz', 'gy')), parts along dimension 4, may hold values from -1.796875 to 1.796875
- solutions: bfloat16 [2, 3, 4, 96, 294912], P(None, None, None, None, ('ta', 'gz', 'gy')), parts along dimension 4, may hold values from -6 to 6
- momenta: int32 [4, 3], replicated, may hold values from -2 to 2
- solution_order: int32 [96], replicated, may hold values from 0 to 95, each once
Outputs:
- meson: float32 [1536, 4, 2, 384], P(('ta', 'gz', 'gy')), parts along dimension 0
The draws below stay inside these ranges and needn't reach their ends.
There are 4 independent parts, one for each index of `ta`. The reference program is written for one: setup_inputs(seed, part) draws one part's arguments, and reference() takes and returns one part's arrays. A program takes and returns all parts, laid end to end along the dimension named above; an argument that names none is the same for every part. Nothing has to cross between parts.
Inputs may be any that keep to these rules, and one draw needn't show every extreme that they name: `solution_order`: each solution appears once.
All inputs are finite; a program needn't handle non-finite values.
Results may differ from the reference program's by a relative error of at most 0.0034.
Values may be sent and summed in bfloat16 or wider, within the bound.
No kernel may reach another device: no remote copies, remote signals or barrier semaphores. Data moves between devices by JAX's collectives and lax.ppermute only.
A program may use at most 192 MiB of HBM per device.

```python
import jax
import jax.numpy as jnp
from jax import lax

NEV = 96
NSOL = 96
NSPIN = 4
NMOM = 4
X = 48
LZ = 48
YD = 3
ZD = 8
NZ = 32
NY = 48
SITES = 73728
N_GZ = 4
N_GY = 16


def plant(result, stream_key, low, high):
    longest = result.shape.index(max(result.shape))
    spots = []
    for shift in (0, 1):
        where = [jax.random.randint(jax.random.fold_in(stream_key, axis), (), 0, length) for axis, length in enumerate(result.shape)]
        where[longest] = (where[longest] + shift) % result.shape[longest]
        spots.append(tuple(where))
    return result.at[spots[0]].set(low).at[spots[1]].set(high)


def spiked(result, key, source, target, blocks, factor):
    owner, partner = [(jnp.arange(result.shape[dim]) // (result.shape[dim] // blocks)).reshape([-1 if axis == dim else 1 for axis in range(result.ndim)]) for dim in (source, target)]
    chosen = jax.random.permutation(key, blocks)[partner]
    strong = (owner == chosen) | (owner == (partner + blocks // 2) % blocks)
    return jnp.where(strong, factor * result, result)


def block_levels(key, shape, cuts, smallest, high):
    def one(dim, shards_of):
        heights = jax.random.uniform(jax.random.fold_in(jax.random.fold_in(key, 6), dim), (shards_of,), jnp.float32, smallest / len(cuts), high / len(cuts))
        return jnp.repeat(jnp.exp(heights), shape[dim] // shards_of).reshape((-1,) + (1,) * (len(shape) - dim - 1))

    factor_of = one(*cuts[0])
    for cut in cuts[1:]:
        factor_of = factor_of * one(*cut)
    return factor_of


def scatter_about(key, dims, deviation, limit, shards=(), held_as=jnp.bfloat16):
    result = deviation * jax.random.normal(key, dims, jnp.float32)
    if shards:
        result = result * block_levels(key, dims, shards, -0.22, 0.18)
    return jnp.clip(result, -limit, limit).astype(held_as)


def noise_with(rng, shape, deviation, limit, shards, heavy, kind=jnp.bfloat16):
    drawn = deviation * jax.random.normal(rng, shape, jnp.float32)
    if shards:
        drawn = drawn * block_levels(rng, shape, shards, -0.22, 0.18)
    return jnp.clip(spiked(drawn, jax.random.fold_in(rng, 3), *heavy), -limit, limit).astype(kind)


def setup_inputs(seed: int = 0, part: int = 0) -> dict:
    seeds = jax.random.split(jax.random.key(seed), 6)
    part_keys = jax.random.split(jax.random.fold_in(seeds[5], part), 6)
    eigenvectors = noise_with(part_keys[0], (2, 3, NEV, SITES), (6 * NZ * NY * X) ** -0.5, 0.015625, ((3, 64),), (3, 2, 32, 2.75))
    gauge_links = scatter_about(part_keys[1], (2, 3, 3, 3, SITES), 0.3, 1.796875, ((4, 64),))
    solutions = scatter_about(part_keys[2], (2, 3, NSPIN, NSOL, SITES), 1.0, 6.0, ((4, 64),))
    momenta = plant(jax.random.randint(seeds[3], (NMOM, 3), -2, 3), jax.random.fold_in(seeds[3], 1), -2, 2).astype(jnp.int32)
    solution_order = jax.random.permutation(seeds[4], NSOL).astype(jnp.int32)
    return {"eigenvectors": eigenvectors, "gauge_links": gauge_links, "solutions": solutions, "momenta": momenta, "solution_order": solution_order}


TWO_PI = 6.283185307179586


def apply_link(link, vector):
    link_real = link[0].astype(jnp.float32)
    link_imag = link[1].astype(jnp.float32)
    vector_real = vector[0].astype(jnp.float32)
    vector_imag = vector[1].astype(jnp.float32)
    out_real = jnp.zeros(vector_real.shape, jnp.float32)
    out_imag = jnp.zeros(vector_real.shape, jnp.float32)
    for colour in range(3):
        entry_real = link_real[:, colour][:, None]
        entry_imag = link_imag[:, colour][:, None]
        out_real = out_real + (entry_real * vector_real[colour][None] - entry_imag * vector_imag[colour][None])
        out_imag = out_imag + (entry_real * vector_imag[colour][None] + entry_imag * vector_real[colour][None])
    return jnp.stack((out_real, out_imag))


def apply_adjoint(link, vector):
    link_real = link[0].astype(jnp.float32)
    link_imag = link[1].astype(jnp.float32)
    vector_real = vector[0].astype(jnp.float32)
    vector_imag = vector[1].astype(jnp.float32)
    out_real = jnp.zeros(vector_real.shape, jnp.float32)
    out_imag = jnp.zeros(vector_real.shape, jnp.float32)
    for colour in range(3):
        entry_real = link_real[colour][:, None]
        entry_imag = link_imag[colour][:, None]
        out_real = out_real + (entry_real * vector_real[colour][None] + entry_imag * vector_imag[colour][None])
        out_imag = out_imag + (entry_real * vector_imag[colour][None] - entry_imag * vector_real[colour][None])
    return jnp.stack((out_real, out_imag))


def phase_table(momenta, slab_index, row_index, column_index, size_z, size_y, size_x):
    x_part = jnp.mod(momenta[:, 0][:, None, None] * column_index[None], size_x).astype(jnp.float32) / size_x
    y_part = jnp.mod(momenta[:, 1][:, None, None] * row_index[None], size_y).astype(jnp.float32) / size_y
    z_part = jnp.mod(momenta[:, 2][:, None, None] * slab_index[None], size_z).astype(jnp.float32) / size_z
    angle = ((x_part + y_part) + z_part) * jnp.float32(TWO_PI)
    return jnp.cos(angle), jnp.sin(angle)


def weighted_rows(field, cosine, sine):
    field_real = field[0][:, None]
    field_imag = field[1][:, None]
    cos_wide = cosine[None, :, None]
    sin_wide = sine[None, :, None]
    rows_real = cos_wide * field_real - sin_wide * field_imag
    rows_imag = cos_wide * field_imag + sin_wide * field_real
    stacked = jnp.stack((rows_real, rows_imag)).astype(jnp.bfloat16)
    return stacked.reshape((2, 3, -1) + stacked.shape[4:])


def lattice_roll(field, step, direction):
    view = field.reshape(field.shape[:-1] + (field.shape[-1] // X, X))
    moved = jnp.roll(view, step, axis=view.ndim - 1 - direction)
    return moved.reshape(field.shape)


def window_shift(field, step):
    depth_axis = field.ndim - 2
    zero_plane = jnp.zeros_like(lax.slice_in_dim(field, 0, 1, axis=depth_axis))
    depth = field.shape[depth_axis]
    if step < 0:
        return jnp.concatenate((lax.slice_in_dim(field, 1, depth, axis=depth_axis), zero_plane), axis=depth_axis)
    return jnp.concatenate((zero_plane, lax.slice_in_dim(field, 0, depth - 1, axis=depth_axis)), axis=depth_axis)


def to_grid(field):
    lead = field.shape[:-1]
    count = len(lead)
    view = field.reshape(lead + (N_GZ, N_GY, ZD, YD, X))
    order = tuple(range(count)) + (count, count + 2, count + 1, count + 3, count + 4)
    moved = jnp.transpose(view, order)
    return moved.reshape(lead + (NZ, NY * X))


def reference(eigenvectors, gauge_links, solutions, momenta, solution_order):
    eigenvectors = to_grid(eigenvectors)
    gauge_links = to_grid(gauge_links)
    solutions = to_grid(solutions)
    slab_index = jnp.arange(NZ, dtype=jnp.int32)[:, None]
    flat_index = jnp.arange(NY * X, dtype=jnp.int32)[None, :]
    cosine, sine = phase_table(momenta, slab_index, flat_index // X, flat_index % X, LZ, NY, X)
    fields = [eigenvectors.astype(jnp.float32)]
    for direction in range(3):
        link = gauge_links[:, direction]
        behind = apply_adjoint(link, eigenvectors).astype(jnp.bfloat16)
        if direction == 2:
            ahead = window_shift(eigenvectors, -1)
            lower = window_shift(behind, 1)
        else:
            ahead = lattice_roll(eigenvectors, -1, direction)
            lower = lattice_roll(behind, 1, direction)
        fields.append(apply_link(link, ahead) - lower.astype(jnp.float32))
    paired = jnp.stack((solutions, jnp.stack((solutions[1], -solutions[0])))).astype(jnp.float32)
    blocks = []
    for field in fields:
        rows_block = weighted_rows(field, cosine, sine).astype(jnp.float32)
        product = lax.dot_general(rows_block, paired, (((0, 1, 3, 4), (1, 2, 5, 6)), ((), ())),
                                  precision=lax.Precision.HIGHEST, preferred_element_type=jnp.float32)
        blocks.append(product)
    summed = jnp.stack(blocks, axis=1)
    ordered = jnp.take(summed, solution_order, axis=4)
    return ordered.reshape(ordered.shape[:3] + (NSPIN * NSOL,))
```

```python
import functools

import jax
import jax.numpy as jnp
from jax import lax
from jax.experimental import pallas as pl
from jax.experimental.pallas import tpu as pltpu
from jax.sharding import PartitionSpec as P

NEV = 96
COLS = 384
X = 48
LZ = 48
YD = 3
ZD = 8
PLANE = YD * X
SITES = ZD * PLANE
TILE = 128
TILES = SITES // TILE
NMOM = 4
EDGE_Y = ZD * X
EDGE_Z = 256
ROWS = 6 * NEV
LINK_ROWS = 32
TWO_PI = 6.283185307179586
F32 = jnp.float32
BF16 = jnp.bfloat16
VMEM = pl.BlockSpec(memory_space=pltpu.VMEM)
SMEM = pl.BlockSpec(memory_space=pltpu.SMEM)
HBM = pl.BlockSpec(memory_space=pl.ANY)
PARAMS = pltpu.CompilerParams(vmem_limit_bytes=56 * 1024 * 1024)


def dot(a, b, dims):
    return lax.dot_general(a, b, (dims, ((), ())), preferred_element_type=F32)


def row_site(column, row):
    return column + (column // X) * (PLANE - X) + row * X


def selector(row):
    sites = lax.broadcasted_iota(jnp.int32, (SITES, EDGE_Y), 0)
    column = lax.broadcasted_iota(jnp.int32, (1, EDGE_Y), 1)
    return (sites == row_site(column, row)).astype(F32).astype(BF16)


def periodic(product, size):
    wrapped = product - size * jnp.floor(product / size)
    return jnp.where(wrapped >= size, wrapped - size, wrapped)


def edge_kernel(place, momenta, vec, link, y_up, y_down, z_up, z_down, phase, flat_link):
    for q in range(18):
        r, mu, a = q // 9, (q // 3) % 3, q % 3
        flat_link[mu * 18 + r * 9 + a * 3 : mu * 18 + r * 9 + a * 3 + 3, :] = link[r, mu, a].astype(F32)
    first, last = selector(0), selector(YD - 1)
    for block in range(6):
        rows = pl.ds(block * NEV, NEV)
        y_up[rows, :] = dot(vec[block], first, ((1,), (0,))).astype(BF16)
        y_down[rows, :] = dot(vec[block], last, ((1,), (0,))).astype(BF16)
        z_up[rows, :] = vec[block, :, :EDGE_Z]
        z_down[rows, :] = vec[block, :, SITES - EDGE_Z :]
    pad = jnp.zeros((LINK_ROWS - 18, SITES), F32)
    y_link = jnp.concatenate((flat_link[18:36, :], pad), axis=0).astype(BF16)
    z_link = jnp.concatenate((flat_link[36:54, :], pad), axis=0).astype(BF16)
    y_down[ROWS:, :] = dot(y_link, last, ((1,), (0,))).astype(BF16)
    z_down[ROWS:, :] = z_link[:, SITES - EDGE_Z :]
    sites = lax.broadcasted_iota(jnp.int32, (8, SITES), 1)
    row = lax.broadcasted_iota(jnp.int32, (8, SITES), 0)
    slab = sites // PLANE
    within = sites - slab * PLANE
    line = within // X
    column = (within - line * X).astype(F32)
    slab = (slab + place[0] * ZD).astype(F32)
    line = (line + place[1] * YD).astype(F32)
    along = [jnp.zeros((8, SITES), F32) for _ in range(3)]
    for p in range(NMOM):
        for axis in range(3):
            along[axis] = jnp.where((row & 3) == p, momenta[p, axis].astype(F32), along[axis])
    x_part = periodic(along[0] * column, float(X)) / X
    y_part = periodic(along[1] * line, float(place_y())) / place_y()
    z_part = periodic(along[2] * slab, float(LZ)) / LZ
    angle = (x_part + y_part + z_part) * F32(TWO_PI)
    phase[...] = jnp.where(row < 4, jnp.cos(angle), jnp.sin(angle))


def place_y():
    return 48


def shift_x(block, step):
    x = lax.broadcasted_iota(jnp.int32, block.shape, 1) % X
    near = pltpu.roll(block, (-step) % SITES, 1)
    far = pltpu.roll(block, (step * (X - 1)) % SITES, 1)
    return jnp.where(x == (X - 1 if step > 0 else 0), far, near)


def shift_y(block, halo, spread, step):
    line = (lax.broadcasted_iota(jnp.int32, block.shape, 1) // X) % YD
    near = pltpu.roll(block, (-step * X) % SITES, 1)
    far = dot(halo, spread, ((1,), (1,)))
    return jnp.where(line == (YD - 1 if step > 0 else 0), far, near)


def shift_z(block, halo, step):
    wide = SITES + EDGE_Z
    if step > 0:
        joined = jnp.concatenate((block, halo), axis=1)
        return pltpu.roll(joined, wide - PLANE, 1)[:, :SITES]
    joined = jnp.concatenate((halo, block), axis=1)
    return pltpu.roll(joined, wide - (EDGE_Z - PLANE), 1)[:, :SITES]


def load_solutions(sol, paired, sems):
    low, high = pl.ds(0, COLS), pl.ds(COLS, COLS)
    copies = [
        pltpu.make_async_copy(sol.at[pl.ds(0, 3)], paired.at[pl.ds(0, 3), low], sems.at[0]),
        pltpu.make_async_copy(sol.at[pl.ds(3, 3)], paired.at[pl.ds(3, 3), low], sems.at[1]),
        pltpu.make_async_copy(sol.at[pl.ds(3, 3)], paired.at[pl.ds(0, 3), high], sems.at[2]),
    ]
    for copy in copies:
        copy.start()
    return copies


def weigh(field, cosine, sine):
    real, imag = field
    return cosine * real - sine * imag, cosine * imag + sine * real


def field_tile(direction, vec, ahead, behind, wide, rows, lanes):
    def tile(ref, block):
        return ref[block, rows, lanes].astype(F32).reshape(2, 8, TILE)

    if direction is None:
        return [(tile(vec, c), tile(vec, 3 + c)) for c in range(3)]
    forward = [(tile(ahead, c), tile(ahead, 3 + c)) for c in range(3)]
    back = [(tile(behind, c), tile(behind, 3 + c)) for c in range(3)]
    fields = []
    for a in range(3):
        real = imag = low_real = low_imag = None
        for b in range(3):
            ur, ui = wide[a * 3 + b, :, lanes], wide[9 + a * 3 + b, :, lanes]
            dr, di = wide[18 + b * 3 + a, :, lanes], wide[27 + b * 3 + a, :, lanes]
            vr, vi = forward[b]
            br, bi = back[b]
            terms = (ur * vr - ui * vi, ur * vi + ui * vr, dr * br + di * bi, dr * bi - di * br)
            if b == 0:
                real, imag, low_real, low_imag = terms
            else:
                real, imag, low_real, low_imag = (
                    real + terms[0], imag + terms[1], low_real + terms[2], low_imag + terms[3])
        fields.append((real - low_real.astype(BF16).astype(F32), imag - low_imag.astype(BF16).astype(F32)))
    return fields


def field_kernel(direction, *refs):
    halos = {None: 0, 0: 0, 1: 2, 2: 2}[direction]
    vec, sol, phase = refs[:3]
    refs = refs[3:]
    link = None
    if direction is not None:
        link, refs = refs[0], refs[1:]
    halo, refs = refs[:halos], refs[halos:]
    out, paired, weighted, total, sems, refs = refs[0], refs[1], refs[2], refs[3], refs[4], refs[5:]
    copies = load_solutions(sol, paired, sems)
    ahead = behind = wide = None
    if direction is not None:
        ahead, behind, wide = refs
        links = link[18 * direction : 18 * direction + 18, :]
        links = jnp.concatenate((links, jnp.zeros((14, SITES), F32)), axis=0)
        if direction == 1:
            up, down = halo
            spread_up, spread_down = selector(YD - 1), selector(0)
        for block in range(6):
            here = vec[block].astype(F32)
            rows = pl.ds(block * NEV, NEV)
            if direction == 0:
                front, rear = shift_x(here, 1), shift_x(here, -1)
            elif direction == 1:
                front = shift_y(here, up[rows, :], spread_up, 1)
                rear = shift_y(here, down[rows, :], spread_down, -1)
            else:
                front = shift_z(here, halo[0][rows, :].astype(F32), 1)
                rear = shift_z(here, halo[1][rows, :].astype(F32), -1)
            ahead[block] = front.astype(BF16)
            behind[block] = rear.astype(BF16)
        if direction == 0:
            links_below = shift_x(links, -1)
        elif direction == 1:
            links_below = shift_y(links, halo[1][ROWS:, :], spread_down, -1)
        else:
            links_below = shift_z(links, halo[1][ROWS:, :].astype(F32), -1)
        for k in range(18):
            wide[k] = jnp.broadcast_to(links[k : k + 1, :], (8, SITES))
            wide[18 + k] = jnp.broadcast_to(links_below[k : k + 1, :], (8, SITES))

    def fill(tile, slot):
        lanes = pl.ds(pl.multiple_of(tile * TILE, TILE), TILE)
        for e in range(NEV // 16):
            fields = field_tile(direction, vec, ahead, behind, wide, pl.ds(e * 16, 16), lanes)
            for p in range(NMOM):
                cosine = jnp.broadcast_to(phase[p : p + 1, lanes], (8, TILE))
                sine = jnp.broadcast_to(phase[4 + p : 5 + p, lanes], (8, TILE))
                for c in range(3):
                    real, imag = weigh(fields[c], cosine, sine)
                    rows = pl.ds(p * NEV + e * 16, 16)
                    weighted[slot, rows, c * TILE : (c + 1) * TILE] = real.reshape(16, TILE).astype(BF16)
                    weighted[slot, rows, (3 + c) * TILE : (4 + c) * TILE] = imag.reshape(16, TILE).astype(BF16)

    def multiply(tile, slot):
        lanes = pl.ds(pl.multiple_of(tile * TILE, TILE), TILE)
        for n in range(3):
            columns = pl.ds(n * 256, 256)
            right = jnp.concatenate([paired[k, columns, lanes] for k in range(6)], axis=1)
            product = dot(weighted[slot], right, ((1,), (1,)))
            total[:, columns] = total[:, columns] + product

    fill(0, 0)
    total[...] = jnp.zeros_like(total)
    for copy in copies:
        copy.wait()
    for c in range(3):
        paired[3 + c, COLS:, :] = -paired[c, :COLS, :]

    def step(i, carry):
        multiply(2 * i, 0)
        fill(2 * i + 1, 1)
        multiply(2 * i + 1, 1)
        fill(2 * i + 2, 0)
        return carry

    lax.fori_loop(0, TILES // 2, step, 0)
    multiply(TILES - 1, 0)
    out[...] = total[...].astype(BF16)


def field_block(direction, vec, sol, phase, link, halo):
    scratch = [
        pltpu.VMEM((6, 2 * COLS, SITES), BF16),
        pltpu.VMEM((2, NMOM * NEV, 6 * TILE), BF16),
        pltpu.VMEM((NMOM * NEV, 2 * COLS), F32),
        pltpu.SemaphoreType.DMA((3,)),
    ]
    args, specs = [vec, sol, phase], [VMEM, HBM, VMEM]
    if direction is not None:
        args += [link, *halo]
        specs += [VMEM] * (1 + len(halo))
        scratch += [pltpu.VMEM((6, NEV, SITES), BF16)] * 2 + [pltpu.VMEM((36, 8, SITES), F32)]
    return pl.pallas_call(
        functools.partial(field_kernel, direction),
        out_shape=jax.ShapeDtypeStruct((NMOM * NEV, 2 * COLS), BF16),
        in_specs=specs,
        out_specs=VMEM,
        scratch_shapes=scratch,
        compiler_params=PARAMS,
        cost_estimate=pl.CostEstimate(flops=2 * 384 * 768 * 6912, bytes_accessed=12_000_000, transcendentals=0),
        name="field_block",
    )(*args)


def middle_kernel(*refs):
    out, held = refs[4], refs[5]
    for g in range(4):
        summed = refs[g][0].astype(F32)
        for m in range(1, 4):
            summed = summed + refs[g][m].astype(F32)
        for owner in range(16):
            held[owner, g * 6 : g * 6 + 6, :] = summed[owner * 6 : owner * 6 + 6, :]
    out[...] = held[...].astype(BF16)


def last_kernel(received, order, out):
    below = lax.broadcasted_iota(jnp.int32, (COLS, COLS), 0)
    moves = (below == order[...]).astype(F32).astype(BF16)
    for r in range(2):
        block = received[:, r * COLS : (r + 1) * COLS]
        moved = dot(block, moves, ((1,), (0,))).reshape(16, 24, COLS)
        summed = jnp.sum(moved, axis=0)
        for g in range(4):
            out[:, 2 * g + r, :] = summed[g * 6 : g * 6 + 6, :]


def call(kernel, shapes, specs, args, name, scratch=()):
    many = isinstance(shapes, list)
    return pl.pallas_call(
        kernel,
        out_shape=shapes,
        in_specs=specs,
        out_specs=[VMEM] * len(shapes) if many else VMEM,
        scratch_shapes=list(scratch),
        compiler_params=PARAMS,
        name=name,
    )(*args)


def body(eigenvectors, gauge_links, solutions, momenta, solution_order):
    vec = eigenvectors.reshape(6, NEV, SITES)
    sol = solutions.reshape(6, COLS, SITES)
    place = jnp.stack((lax.axis_index("gz"), lax.axis_index("gy"))).astype(jnp.int32)
    order = (jnp.tile(solution_order, 4) + (jnp.arange(COLS) // NEV) * NEV).astype(jnp.int32)[None, :]
    shape = jax.ShapeDtypeStruct
    y_up, y_down, z_up, z_down, phase, link = call(
        edge_kernel,
        [
            shape((ROWS, EDGE_Y), BF16),
            shape((ROWS + LINK_ROWS, EDGE_Y), BF16),
            shape((ROWS, EDGE_Z), BF16),
            shape((ROWS + LINK_ROWS, EDGE_Z), BF16),
            shape((8, SITES), F32),
            shape((54, SITES), F32),
        ],
        [SMEM, SMEM, VMEM, VMEM],
        (place, momenta, vec, gauge_links),
        "edges",
    )
    size = lax.axis_size("gy")
    y_up = lax.ppermute(y_up, "gy", [(i, (i - 1) % size) for i in range(size)])
    y_down = lax.ppermute(y_down, "gy", [(i, (i + 1) % size) for i in range(size)])
    size = lax.axis_size("gz")
    z_up = lax.ppermute(z_up, "gz", [(i, i - 1) for i in range(1, size)])
    z_down = lax.ppermute(z_down, "gz", [(i, i + 1) for i in range(size - 1)])
    halos = ((), (), (y_up, y_down), (z_up, z_down))
    parts = []
    for g in range(4):
        block = field_block(None if g == 0 else g - 1, vec, sol, phase, link, halos[g])
        moved = lax.all_to_all(block, "gz", 0, 0, tiled=True)
        parts.append(moved.reshape(4, NEV, 2 * COLS))
    middle = call(
        middle_kernel,
        shape((16, 24, 2 * COLS), BF16),
        [VMEM] * 4,
        parts,
        "middle",
        [pltpu.VMEM((16, 24, 2 * COLS), F32)],
    )
    received = lax.all_to_all(middle, "gy", 0, 0, tiled=True)
    out = call(
        last_kernel,
        shape((6, 8, COLS), F32),
        [VMEM, VMEM],
        (received.reshape(16 * 24, 2 * COLS), order),
        "last",
    )
    return out.reshape(6, 4, 2, COLS)


def solution(mesh):
    return jax.shard_map(
        body,
        mesh=mesh,
        in_specs=(
            P(None, None, None, ("ta", "gz", "gy")),
            P(None, None, None, None, ("ta", "gz", "gy")),
            P(None, None, None, None, ("ta", "gz", "gy")),
            P(),
            P(),
        ),
        out_specs=P(("ta", "gz", "gy"), None, None, None),
        check_vma=False,
    )
```

```python
import functools

import jax
import jax.numpy as jnp
from jax import lax
from jax.experimental import pallas as pl
from jax.experimental.pallas import tpu as pltpu
from jax.sharding import PartitionSpec as P

NEV = 96
COLS = 384
X = 48
LZ = 48
NY = 48
YD = 3
ZD = 8
PLANE = YD * X
SITES = ZD * PLANE
TILE = 128
TILES = SITES // TILE
NMOM = 4
EDGE_Y = ZD * X
EDGE_Z = 256
ROWS = 6 * NEV
LINK_ROWS = 32
TWO_PI = 6.283185307179586
F32 = jnp.float32
BF16 = jnp.bfloat16
VMEM = pl.BlockSpec(memory_space=pltpu.VMEM)
SMEM = pl.BlockSpec(memory_space=pltpu.SMEM)
HBM = pl.BlockSpec(memory_space=pltpu.HBM)
PARAMS = pltpu.CompilerParams(vmem_limit_bytes=30 * 1024 * 1024)


def dot(a, b, dims):
    return lax.dot_general(a, b, (dims, ((), ())), preferred_element_type=F32)


def row_site(column, row):
    return column + (column // X) * (PLANE - X) + row * X


def selector(row):
    sites = lax.broadcasted_iota(jnp.int32, (SITES, EDGE_Y), 0)
    column = lax.broadcasted_iota(jnp.int32, (1, EDGE_Y), 1)
    return (sites == row_site(column, row)).astype(F32).astype(BF16)


def periodic(product, size):
    wrapped = product - size * jnp.floor(product / size)
    return jnp.where(wrapped >= size, wrapped - size, wrapped)


def wave(turns):
    quarter = jnp.floor(turns * 4.0 + 0.5)
    angle = (turns - quarter * 0.25) * F32(TWO_PI)
    square = angle * angle
    cosine = 1.0 + square * (-0.5 + square * (1 / 24 + square * (-1 / 720 + square * (1 / 40320))))
    sine = angle * (1.0 + square * (-1 / 6 + square * (1 / 120 + square * (-1 / 5040 + square * (1 / 362880)))))
    quadrant = quarter.astype(jnp.int32) & 3
    odd = (quadrant & 1) == 1
    sign_cosine = jnp.where((quadrant == 1) | (quadrant == 2), -1.0, 1.0)
    sign_sine = jnp.where(quadrant >= 2, -1.0, 1.0)
    return jnp.where(odd, sine, cosine) * sign_cosine, jnp.where(odd, cosine, sine) * sign_sine


def prepare_kernel(place, momenta, vec_hbm, link, y_up, y_down, z_up, z_down, phase, flat_link, vec, first_row, last_row, sem):
    fetch = pltpu.make_async_copy(vec_hbm, vec, sem)
    fetch.start()
    for q in range(27):
        flat_link[2 * q : 2 * q + 2, :] = link[q // 9, (q // 3) % 3, q % 3].astype(F32)
    sites = lax.broadcasted_iota(jnp.int32, (8, SITES), 1)
    row = lax.broadcasted_iota(jnp.int32, (8, SITES), 0)
    slab = sites // PLANE
    within = sites - slab * PLANE
    line = within // X
    column = (within - line * X).astype(F32)
    slab = (slab + place[0] * ZD).astype(F32)
    line = (line + place[1] * YD).astype(F32)
    along = [jnp.zeros((8, SITES), F32) for _ in range(3)]
    for p in range(NMOM):
        for axis in range(3):
            value = momenta[(place[0] + p) & 3, axis].astype(F32)
            along[axis] = jnp.where((row & 3) == p, value, along[axis])
    x_part = periodic(along[0] * column, float(X)) / X
    y_part = periodic(along[1] * line, float(NY)) / NY
    z_part = periodic(along[2] * slab, float(LZ)) / LZ
    cosine, sine = wave(x_part + y_part + z_part)
    table = jnp.where(row < 4, cosine, sine)
    for k in range(8):
        phase[k] = jnp.broadcast_to(table[k : k + 1, :], (8, SITES))
    first_row[...] = selector(0)
    last_row[...] = selector(YD - 1)
    first, last = first_row[...], last_row[...]
    pad = jnp.zeros((LINK_ROWS - 18, SITES), F32)
    y_link = jnp.concatenate((flat_link[18:36, :], pad), axis=0).astype(BF16)
    z_link = jnp.concatenate((flat_link[36:54, :], pad), axis=0).astype(BF16)
    y_down[ROWS:, :] = dot(y_link, last, ((1,), (0,))).astype(BF16)
    z_down[ROWS:, :] = z_link[:, SITES - EDGE_Z :]
    fetch.wait()
    for block in range(6):
        rows = pl.ds(block * NEV, NEV)
        y_up[rows, :] = dot(vec[block], first, ((1,), (0,))).astype(BF16)
        y_down[rows, :] = dot(vec[block], last, ((1,), (0,))).astype(BF16)
        z_up[rows, :] = vec[block, :, :EDGE_Z]
        z_down[rows, :] = vec[block, :, SITES - EDGE_Z :]


def choose(mask, yes, no):
    parts = (yes.shape[0] // 8, 8, SITES)
    return jnp.where(mask[None], yes.reshape(parts), no.reshape(parts)).reshape(yes.shape)


def shift_x(block, step):
    x = lax.broadcasted_iota(jnp.int32, (8, SITES), 1) % X
    near = pltpu.roll(block, (-step) % SITES, 1)
    far = pltpu.roll(block, (step * (X - 1)) % SITES, 1)
    return choose(x == (X - 1 if step > 0 else 0), far, near)


def shift_y(block, halo, spread, step):
    line = (lax.broadcasted_iota(jnp.int32, (8, SITES), 1) // X) % YD
    near = pltpu.roll(block, (-step * X) % SITES, 1)
    far = dot(halo, spread, ((1,), (1,)))
    return choose(line == (YD - 1 if step > 0 else 0), far, near)


def shift_z(block, halo, step):
    wide = SITES + EDGE_Z
    if step > 0:
        joined = jnp.concatenate((block, halo), axis=1)
        return pltpu.roll(joined, wide - PLANE, 1)[:, :SITES]
    joined = jnp.concatenate((halo, block), axis=1)
    return pltpu.roll(joined, wide - (EDGE_Z - PLANE), 1)[:, :SITES]


def weigh(field, cosine, sine):
    real, imag = field
    return cosine * real - sine * imag, cosine * imag + sine * real


def field_tile(direction, vec, ahead, behind, wide, rows, lanes):
    def tile(ref, block):
        return ref[block, rows, lanes].astype(F32).reshape(2, 8, TILE)

    if direction is None:
        return [(tile(vec, c), tile(vec, 3 + c)) for c in range(3)]
    forward = [(tile(ahead, c), tile(ahead, 3 + c)) for c in range(3)]
    back = [(tile(behind, c), tile(behind, 3 + c)) for c in range(3)]
    fields = []
    for a in range(3):
        real = imag = low_real = low_imag = None
        for b in range(3):
            ahead_at, behind_at = 2 * (a * 3 + b), 18 + 2 * (b * 3 + a)
            ur, ui = wide[ahead_at, :, lanes], wide[ahead_at + 1, :, lanes]
            dr, di = wide[behind_at, :, lanes], wide[behind_at + 1, :, lanes]
            vr, vi = forward[b]
            br, bi = back[b]
            terms = (ur * vr - ui * vi, ur * vi + ui * vr, dr * br + di * bi, dr * bi - di * br)
            if b == 0:
                real, imag, low_real, low_imag = terms
            else:
                real, imag, low_real, low_imag = (
                    real + terms[0], imag + terms[1], low_real + terms[2], low_imag + terms[3])
        fields.append((real - low_real.astype(BF16).astype(F32), imag - low_imag.astype(BF16).astype(F32)))
    return fields


def shift_all(direction, vec, link, halo, ahead, behind, wide):
    links = link[18 * direction : 18 * direction + 18, :]
    links = jnp.concatenate((links, jnp.zeros((14, SITES), F32)), axis=0)
    for block in range(6):
        here = vec[block].astype(F32)
        rows = pl.ds(block * NEV, NEV)
        if direction == 0:
            front, rear = shift_x(here, 1), shift_x(here, -1)
        elif direction == 1:
            front = shift_y(here, halo[0][rows, :], halo[3][...], 1)
            rear = shift_y(here, halo[1][rows, :], halo[2][...], -1)
        else:
            front = shift_z(here, halo[0][rows, :].astype(F32), 1)
            rear = shift_z(here, halo[1][rows, :].astype(F32), -1)
        ahead[block] = front.astype(BF16)
        behind[block] = rear.astype(BF16)
    if direction == 0:
        links_below = shift_x(links, -1)
    elif direction == 1:
        links_below = shift_y(links, halo[1][ROWS:, :], halo[2][...], -1)
    else:
        links_below = shift_z(links, halo[1][ROWS:, :].astype(F32), -1)
    for k in range(18):
        wide[k] = jnp.broadcast_to(links[k : k + 1, :], (8, SITES))
        wide[18 + k] = jnp.broadcast_to(links_below[k : k + 1, :], (8, SITES))


def field_kernel(directions, *refs):
    refs = list(refs)
    vec, sol, phase, link = [refs.pop(0) for _ in range(4)]
    halos = [[refs.pop(0) for _ in range(HALOS[d])] for d in directions]
    outs = [refs.pop(0) for _ in range(NMOM)]
    negated, weighted, total = [refs.pop(0) for _ in range(3)]
    shifted = [[refs.pop(0) for _ in range(0 if d is None else 3)] for d in directions]
    for c in range(3):
        negated[c] = -sol[c]
    for d, halo, place in zip(directions, halos, shifted):
        if d is not None:
            shift_all(d, vec, link, halo, *place)

    def fill(tile, slot, part):
        lanes = pl.ds(tile * TILE, TILE)
        for e in range(2 * part, 2 * part + 2):
            for f, d in enumerate(directions):
                ahead, behind, wide = shifted[f] if shifted[f] else (None, None, None)
                fields = field_tile(d, vec, ahead, behind, wide, pl.ds(e * 16, 16), lanes)
                for p in range(NMOM):
                    cosine, sine = phase[p, :, lanes], phase[4 + p, :, lanes]
                    rows = pl.ds((p * len(directions) + f) * NEV + e * 16, 16)
                    for c in range(3):
                        real, imag = weigh(fields[c], cosine, sine)
                        weighted[slot, rows, c * TILE : (c + 1) * TILE] = real.reshape(16, TILE).astype(BF16)
                        weighted[slot, rows, (3 + c) * TILE : (4 + c) * TILE] = imag.reshape(16, TILE).astype(BF16)

    def right_hand(lanes, k, first, stop):
        pieces = []
        if first < COLS:
            pieces.append(sol[k, first : min(stop, COLS), lanes])
        if stop > COLS:
            rows = slice(max(first, COLS) - COLS, stop - COLS)
            pieces.append(sol[3 + k, rows, lanes] if k < 3 else negated[k - 3, rows, lanes])
        return pieces[0] if len(pieces) == 1 else jnp.concatenate(pieces, axis=0)

    def multiply(tile, slot, part):
        lanes = pl.ds(tile * TILE, TILE)
        columns = pl.ds(part * 256, 256)
        right = jnp.concatenate([right_hand(lanes, k, part * 256, part * 256 + 256) for k in range(6)], axis=1)
        product = dot(weighted[slot], right, ((1,), (1,)))
        total[:, columns] = product if tile == 0 else total[:, columns] + product

    for part in range(3):
        fill(0, 0, part)
    for tile in range(TILES):
        for part in range(3):
            multiply(tile, tile % 2, part)
            if tile + 1 < TILES:
                fill(tile + 1, (tile + 1) % 2, part)
    height = NEV * len(directions)
    for p in range(NMOM):
        outs[p][...] = total[p * height : (p + 1) * height, :].astype(BF16)


HALOS = {None: 0, 0: 0, 1: 4, 2: 2}


def field_block(directions, vec, sol, phase, link, halos):
    height = NEV * len(directions)
    scratch = [
        pltpu.VMEM((3, COLS, SITES), BF16),
        pltpu.VMEM((2, NMOM * height, 6 * TILE), BF16),
        pltpu.VMEM((NMOM * height, 2 * COLS), F32),
    ]
    args = [vec, sol, phase, link, *halos]
    for d in directions:
        if d is not None:
            scratch += [pltpu.VMEM((6, NEV, SITES), BF16)] * 2 + [pltpu.VMEM((36, 8, SITES), F32)]
    return pl.pallas_call(
        functools.partial(field_kernel, directions),
        out_shape=[jax.ShapeDtypeStruct((height, 2 * COLS), BF16)] * NMOM,
        in_specs=[VMEM] * len(args),
        out_specs=[VMEM] * NMOM,
        scratch_shapes=scratch,
        compiler_params=PARAMS,
        cost_estimate=pl.CostEstimate(
            flops=16 * 384 * 768 * 6912, bytes_accessed=12_000_000, transcendentals=0),
        name="field_block",
    )(*args)


def middle_kernel(place, *refs):
    outs, held = refs[8:12], refs[12]
    for pair in range(2):
        summed = refs[4 * pair][...].astype(F32)
        for m in range(1, 4):
            summed = summed + refs[4 * pair + m][...].astype(F32)
        for f in range(2):
            g = 2 * pair + f
            for owner in range(16):
                held[owner, g * 6 : g * 6 + 6, :] = summed[f * NEV + owner * 6 : f * NEV + owner * 6 + 6, :]
    low = place[1] & 3
    for m in range(4):
        for q in range(4):
            outs[m][q] = held[q * 4 + (low ^ m)].astype(BF16)


def second_kernel(place, own, one, two, three, *outs):
    high = place[1] // 4
    for d in range(4):
        at = (high + d) & 3
        summed = own[at].astype(F32)
        for ref in (one, two, three):
            summed = summed + ref[at].astype(F32)
        outs[d][...] = summed.astype(outs[d].dtype)


def last_kernel(own, one, two, three, order, out):
    below = lax.broadcasted_iota(jnp.int32, (COLS, COLS), 0)
    moves = (below == order[...]).astype(F32).astype(BF16)
    summed = own[...]
    for ref in (one, two, three):
        summed = summed + ref[...].astype(F32)
    for r in range(2):
        rest = summed[:, r * COLS : (r + 1) * COLS]
        moved = None
        for _ in range(3):
            part = rest.astype(BF16)
            rest = rest - part.astype(F32)
            term = dot(part, moves, ((1,), (0,)))
            moved = term if moved is None else moved + term
        for g in range(4):
            out[:, g, r, :] = moved[g * 6 : g * 6 + 6, :]


def call(kernel, shapes, specs, args, name, scratch=()):
    many = isinstance(shapes, list)
    return pl.pallas_call(
        kernel,
        out_shape=shapes,
        in_specs=specs,
        out_specs=[VMEM] * len(shapes) if many else VMEM,
        scratch_shapes=list(scratch),
        compiler_params=PARAMS,
        name=name,
    )(*args)


def prepare(place, momenta, vec, gauge_links):
    shape = jax.ShapeDtypeStruct
    made = call(
        prepare_kernel,
        [
            shape((ROWS, EDGE_Y), BF16),
            shape((ROWS + LINK_ROWS, EDGE_Y), BF16),
            shape((ROWS, EDGE_Z), BF16),
            shape((ROWS + LINK_ROWS, EDGE_Z), BF16),
            pltpu.VMEM((8, 8, SITES), F32),
            pltpu.VMEM((54, SITES), F32),
            pltpu.VMEM((6, NEV, SITES), BF16),
            pltpu.VMEM((SITES, EDGE_Y), BF16),
            pltpu.VMEM((SITES, EDGE_Y), BF16),
        ],
        [SMEM, SMEM, HBM, VMEM],
        (
            place,
            momenta,
            pltpu.with_memory_space_constraint(vec, pltpu.HBM),
            jnp.transpose(gauge_links, (1, 2, 3, 0, 4)),
        ),
        "prepare",
        [pltpu.SemaphoreType.DMA(())],
    )
    return [*made[:4], *(pltpu.with_memory_space_constraint(a, pltpu.VMEM) for a in made[4:])]


def body(eigenvectors, gauge_links, solutions, momenta, solution_order):
    vec = eigenvectors.reshape(6, NEV, SITES)
    sol = solutions.reshape(6, COLS, SITES)
    place = jnp.stack((lax.axis_index("gz"), lax.axis_index("gy"))).astype(jnp.int32)
    order = (jnp.tile(solution_order, 4) + (jnp.arange(COLS) // NEV) * NEV).astype(jnp.int32)[None, :]
    y_up, y_down, z_up, z_down, phase, link, vec, first, last = prepare(place, momenta, vec, gauge_links)
    sol = pltpu.with_memory_space_constraint(sol, pltpu.VMEM)
    size = lax.axis_size("gy")
    y_up = lax.ppermute(y_up, "gy", [(i, (i - 1) % size) for i in range(size)])
    y_down = lax.ppermute(y_down, "gy", [(i, (i + 1) % size) for i in range(size)])
    slabs = lax.axis_size("gz")
    z_up = lax.ppermute(z_up, "gz", [(i, i - 1) for i in range(1, slabs)])
    z_down = lax.ppermute(z_down, "gz", [(i, i + 1) for i in range(slabs - 1)])
    parts = []
    for directions, halos in (((None, 0), ()), ((1, 2), (y_up, y_down, first, last, z_up, z_down))):
        blocks = field_block(directions, vec, sol, phase, link, halos)
        parts.append(blocks[0])
        for k in range(1, 4):
            parts.append(lax.ppermute(blocks[k], "gz", [(i, (i + k) % slabs) for i in range(slabs)]))
    shape = jax.ShapeDtypeStruct
    blocks = call(
        middle_kernel,
        [shape((4, 24, 2 * COLS), BF16)] * 4,
        [SMEM] + [VMEM] * 8,
        (place, *parts),
        "middle",
        [pltpu.VMEM((16, 24, 2 * COLS), F32)],
    )
    parts = [blocks[0]]
    for m in range(1, 4):
        parts.append(lax.ppermute(blocks[m], "gy", [(i, i ^ m) for i in range(size)]))
    blocks = call(
        second_kernel,
        [shape((24, 2 * COLS), F32)] + [shape((24, 2 * COLS), BF16)] * 3,
        [SMEM] + [VMEM] * 4,
        (place, *parts),
        "second",
    )
    parts = [blocks[0]]
    for d in range(1, 4):
        parts.append(lax.ppermute(blocks[d], "gy", [(i, (i + 4 * d) % size) for i in range(size)]))
    return call(
        last_kernel,
        shape((6, 4, 2, COLS), F32),
        [VMEM] * 5,
        (*parts, order),
        "last",
    )


def solution(mesh):
    return jax.shard_map(
        body,
        mesh=mesh,
        in_specs=(
            P(None, None, None, ("ta", "gz", "gy")),
            P(None, None, None, None, ("ta", "gz", "gy")),
            P(None, None, None, None, ("ta", "gz", "gy")),
            P(),
            P(),
        ),
        out_specs=P(("ta", "gz", "gy"), None, None, None),
        check_vma=False,
    )
```

```python
import functools

import jax
import jax.numpy as jnp
from jax import lax
from jax.experimental import pallas as pl
from jax.experimental.pallas import tpu as pltpu
from jax.sharding import PartitionSpec as P

NEV = 96
COLS = 384
X = 48
LZ = 48
NY = 48
YD = 3
ZD = 8
PLANE = YD * X
SITES = ZD * PLANE
TILE = 128
TILES = SITES // TILE
NMOM = 4
NZ_DEVICES = 4
EDGE_Y = ZD * X
EDGE_Z = 256
ROWS = 6 * NEV
LINK_ROWS = 32
TWO_PI = 6.283185307179586
F32 = jnp.float32
BF16 = jnp.bfloat16
VMEM = pl.BlockSpec(memory_space=pltpu.VMEM)
SMEM = pl.BlockSpec(memory_space=pltpu.SMEM)
HBM = pl.BlockSpec(memory_space=pltpu.HBM)
PARAMS = pltpu.CompilerParams(vmem_limit_bytes=30 * 1024 * 1024)


def dot(a, b, dims):
    return lax.dot_general(a, b, (dims, ((), ())), preferred_element_type=F32)


def row_site(column, row):
    return column + (column // X) * (PLANE - X) + row * X


def selector(row):
    sites = lax.broadcasted_iota(jnp.int32, (SITES, EDGE_Y), 0)
    column = lax.broadcasted_iota(jnp.int32, (1, EDGE_Y), 1)
    return (sites == row_site(column, row)).astype(F32).astype(BF16)


def periodic(product, size):
    wrapped = product - size * jnp.floor(product / size)
    return jnp.where(wrapped >= size, wrapped - size, wrapped)


def wave(turns):
    quarter = jnp.floor(turns * 4.0 + 0.5)
    angle = (turns - quarter * 0.25) * F32(TWO_PI)
    square = angle * angle
    cosine = 1.0 + square * (-0.5 + square * (1 / 24 + square * (-1 / 720 + square * (1 / 40320))))
    sine = angle * (1.0 + square * (-1 / 6 + square * (1 / 120 + square * (-1 / 5040 + square * (1 / 362880)))))
    quadrant = quarter.astype(jnp.int32) & 3
    odd = (quadrant & 1) == 1
    sign_cosine = jnp.where((quadrant == 1) | (quadrant == 2), -1.0, 1.0)
    sign_sine = jnp.where(quadrant >= 2, -1.0, 1.0)
    return jnp.where(odd, sine, cosine) * sign_cosine, jnp.where(odd, cosine, sine) * sign_sine


def prepare_kernel(
    place, momenta_hbm, vec_hbm, link_hbm, sol_hbm,
    y_up, y_down, phase, flat_link, vec, first_row, last_row, sol,
    momenta, link, sems,
):
    fetches = [
        pltpu.make_async_copy(link_hbm, link, sems.at[0]),
        pltpu.make_async_copy(momenta_hbm, momenta, sems.at[1]),
        pltpu.make_async_copy(vec_hbm, vec, sems.at[2]),
        pltpu.make_async_copy(sol_hbm, sol, sems.at[3]),
    ]
    for fetch in fetches:
        fetch.start()
    first_row[...] = selector(0)
    last_row[...] = selector(YD - 1)
    first, last = first_row[...], last_row[...]
    fetches[0].wait()
    for q in range(27):
        flat_link[2 * q : 2 * q + 2, :] = link[q // 9, (q // 3) % 3, q % 3].astype(F32)
    pad = jnp.zeros((LINK_ROWS - 18, SITES), F32)
    y_link = jnp.concatenate((flat_link[18:36, :], pad), axis=0).astype(BF16)
    y_down[ROWS:, :] = dot(y_link, last, ((1,), (0,))).astype(BF16)
    fetches[1].wait()
    sites = lax.broadcasted_iota(jnp.int32, (8, SITES), 1)
    row = lax.broadcasted_iota(jnp.int32, (8, SITES), 0)
    slab = sites // PLANE
    within = sites - slab * PLANE
    line = within // X
    column = (within - line * X).astype(F32)
    slab = (slab + place[0] * ZD).astype(F32)
    line = (line + place[1] * YD).astype(F32)
    along = [jnp.zeros((8, SITES), F32) for _ in range(3)]
    for p in range(NMOM):
        for axis in range(3):
            value = momenta[(place[0] + p) & 3, axis].astype(F32)
            along[axis] = jnp.where((row & 3) == p, value, along[axis])
    x_part = periodic(along[0] * column, float(X)) / X
    y_part = periodic(along[1] * line, float(NY)) / NY
    z_part = periodic(along[2] * slab, float(LZ)) / LZ
    cosine, sine = wave(x_part + y_part + z_part)
    table = jnp.where(row < 4, cosine, sine)
    for k in range(8):
        phase[k] = jnp.broadcast_to(table[k : k + 1, :], (8, SITES))
    fetches[2].wait()
    for block in range(6):
        rows = pl.ds(block * NEV, NEV)
        y_up[rows, :] = dot(vec[block], first, ((1,), (0,))).astype(BF16)
        y_down[rows, :] = dot(vec[block], last, ((1,), (0,))).astype(BF16)
    fetches[3].wait()


def choose(mask, yes, no):
    parts = (yes.shape[0] // 8, 8, SITES)
    return jnp.where(mask[None], yes.reshape(parts), no.reshape(parts)).reshape(yes.shape)


def shift_x(block, step):
    x = lax.broadcasted_iota(jnp.int32, (8, SITES), 1) % X
    near = pltpu.roll(block, (-step) % SITES, 1)
    far = pltpu.roll(block, (step * (X - 1)) % SITES, 1)
    return choose(x == (X - 1 if step > 0 else 0), far, near)


def shift_y(block, halo, spread, step):
    line = (lax.broadcasted_iota(jnp.int32, (8, SITES), 1) // X) % YD
    near = pltpu.roll(block, (-step * X) % SITES, 1)
    far = dot(halo, spread, ((1,), (1,)))
    return choose(line == (YD - 1 if step > 0 else 0), far, near)


def shift_z(block, halo, step):
    wide = SITES + EDGE_Z
    if step > 0:
        joined = jnp.concatenate((block, halo), axis=1)
        return pltpu.roll(joined, wide - PLANE, 1)[:, :SITES]
    joined = jnp.concatenate((halo, block), axis=1)
    return pltpu.roll(joined, wide - (EDGE_Z - PLANE), 1)[:, :SITES]


def weigh(field, cosine, sine):
    real, imag = field
    return cosine * real - sine * imag, cosine * imag + sine * real


def rounded(block):
    return block.reshape(16, TILE).astype(BF16).astype(F32).reshape(2, 8, TILE)


def field_tile(direction, vec, ahead, behind, wide, rows, lanes):
    def tile(ref, block):
        return ref[block, rows, lanes].astype(F32).reshape(2, 8, TILE)

    if direction is None:
        return [(tile(vec, c), tile(vec, 3 + c)) for c in range(3)]
    forward = [(tile(ahead, c), tile(ahead, 3 + c)) for c in range(3)]
    back = [(tile(behind, c), tile(behind, 3 + c)) for c in range(3)]
    fields = []
    for a in range(3):
        real = imag = low_real = low_imag = None
        for b in range(3):
            ahead_at, behind_at = 2 * (a * 3 + b), 18 + 2 * (b * 3 + a)
            ur, ui = wide[ahead_at, :, lanes], wide[ahead_at + 1, :, lanes]
            dr, di = wide[behind_at, :, lanes], wide[behind_at + 1, :, lanes]
            vr, vi = forward[b]
            br, bi = back[b]
            terms = (ur * vr - ui * vi, ur * vi + ui * vr, dr * br + di * bi, dr * bi - di * br)
            if b == 0:
                real, imag, low_real, low_imag = terms
            else:
                real, imag, low_real, low_imag = (
                    real + terms[0], imag + terms[1], low_real + terms[2], low_imag + terms[3])
        fields.append((real - rounded(low_real), imag - rounded(low_imag)))
    return fields


def shift_all(direction, place, vec, link, halo, ahead, behind, wide):
    links = link[18 * direction : 18 * direction + 18, :]
    links = jnp.concatenate((links, jnp.zeros((14, SITES), F32)), axis=0)
    if direction == 2:
        keep_up = (place[0] < NZ_DEVICES - 1).astype(F32)
        keep_down = (place[0] > 0).astype(F32)
    for block in range(6):
        here = vec[block].astype(F32)
        rows = pl.ds(block * NEV, NEV)
        if direction == 0:
            front, rear = shift_x(here, 1), shift_x(here, -1)
        elif direction == 1:
            front = shift_y(here, halo[0][rows, :], halo[3][...], 1)
            rear = shift_y(here, halo[1][rows, :], halo[2][...], -1)
        else:
            rows = slice(2 * NEV + block % 2 * NEV, 3 * NEV + block % 2 * NEV)
            columns = slice(block // 2 * EDGE_Z, block // 2 * EDGE_Z + EDGE_Z)
            front = shift_z(here, halo[0][rows, columns].astype(F32) * keep_up, 1)
            rear = shift_z(here, halo[1][rows, columns].astype(F32) * keep_down, -1)
        ahead[block] = front.astype(BF16)
        behind[block] = rear.astype(BF16)
    if direction == 0:
        links_below = shift_x(links, -1)
    elif direction == 1:
        links_below = shift_y(links, halo[1][ROWS:, :], halo[2][...], -1)
    else:
        links_below = shift_z(links, halo[1][4 * NEV :, :EDGE_Z].astype(F32) * keep_down, -1)
    for k in range(18):
        wide[k] = jnp.broadcast_to(links[k : k + 1, :], (8, SITES))
        wide[18 + k] = jnp.broadcast_to(links_below[k : k + 1, :], (8, SITES))


def field_kernel(directions, *refs):
    refs = list(refs)
    place, vec, sol, phase, link = [refs.pop(0) for _ in range(5)]
    halos = [[refs.pop(0) for _ in range(HALOS[d])] for d in directions]
    outs = [refs.pop(0) for _ in range(NMOM)]
    height = NEV * len(directions)
    leads = directions[0] is None
    if leads:
        negated = refs.pop(0)
    else:
        negated = halos[-1].pop()
    if 1 in directions:
        outs[2][NEV:, :] = halos[0].pop()[...]
    weighted, total = [refs.pop(0) for _ in range(2)]
    shifted = [[refs.pop(0) for _ in range(0 if d is None else 3)] for d in directions]
    for d, halo, kept in zip(directions, halos, shifted):
        if d is not None:
            shift_all(d, place, vec, link, halo, *kept)

    def fill(tile, slot, part):
        lanes = pl.ds(tile * TILE, TILE)
        for e in range(2 * part, 2 * part + 2):
            for f, d in enumerate(directions):
                ahead, behind, wide = shifted[f] if shifted[f] else (None, None, None)
                fields = field_tile(d, vec, ahead, behind, wide, pl.ds(e * 16, 16), lanes)
                for p in range(NMOM):
                    cosine, sine = phase[p, :, lanes], phase[4 + p, :, lanes]
                    rows = pl.ds((p * len(directions) + f) * NEV + e * 16, 16)
                    for c in range(3):
                        real, imag = weigh(fields[c], cosine, sine)
                        weighted[slot, rows, c * TILE : (c + 1) * TILE] = real.reshape(16, TILE).astype(BF16)
                        weighted[slot, rows, (3 + c) * TILE : (4 + c) * TILE] = imag.reshape(16, TILE).astype(BF16)

    def right_hand(lanes, k, first, stop):
        pieces = []
        if first < COLS:
            pieces.append(sol[k, first : min(stop, COLS), lanes])
        if stop > COLS:
            rows = slice(max(first, COLS) - COLS, stop - COLS)
            pieces.append(sol[3 + k, rows, lanes] if k < 3 else negated[k - 3, rows, lanes])
        return pieces[0] if len(pieces) == 1 else jnp.concatenate(pieces, axis=0)

    def multiply(tile, slot, part):
        lanes = pl.ds(tile * TILE, TILE)
        columns = pl.ds(part * 256, 256)
        right = jnp.concatenate([right_hand(lanes, k, part * 256, part * 256 + 256) for k in range(6)], axis=1)
        product = dot(weighted[slot], right, ((1,), (1,)))
        total[:, columns] = product if tile == 0 else total[:, columns] + product

    for part in range(3):
        fill(0, 0, part)
    if leads:
        for c in range(3):
            negated[c] = -sol[c]
        for third in range(3):
            columns = slice(third * EDGE_Z, third * EDGE_Z + EDGE_Z)
            for b in range(2):
                at = slice(height + b * NEV, height + b * NEV + NEV)
                outs[3][at, columns] = vec[2 * third + b, :, :EDGE_Z]
                outs[1][at, columns] = vec[2 * third + b, :, SITES - EDGE_Z :]
        z_link = jnp.concatenate((link[36:54, SITES - EDGE_Z :], jnp.zeros((LINK_ROWS - 18, EDGE_Z), F32)), axis=0)
        outs[1][height + 2 * NEV :, :EDGE_Z] = z_link.astype(BF16)
        outs[1][height + 2 * NEV :, EDGE_Z:] = jnp.zeros((LINK_ROWS, 2 * EDGE_Z), BF16)
    for tile in range(TILES):
        for part in range(3):
            multiply(tile, tile % 2, part)
            if tile + 1 < TILES:
                fill(tile + 1, (tile + 1) % 2, part)
    for p in range(NMOM):
        outs[p][:height, :] = total[p * height : (p + 1) * height, :].astype(BF16)


HALOS = {None: 0, 0: 0, 1: 6, 2: 3}


def field_block(directions, place, vec, sol, phase, link, halos):
    height = NEV * len(directions)
    leads = directions[0] is None
    scratch = [
        pltpu.VMEM((2, NMOM * height, 6 * TILE), BF16),
        pltpu.VMEM((NMOM * height, 2 * COLS), F32),
    ]
    args = [place, vec, sol, phase, link, *halos]
    specs = [SMEM] + [VMEM] * (len(args) - 1)
    for d in directions:
        if d is not None:
            scratch += [pltpu.VMEM((6, NEV, SITES), BF16)] * 2 + [pltpu.VMEM((36, 8, SITES), F32)]
    tall = [2 * NEV + LINK_ROWS, 0, 2 * NEV] if leads else [0, 2 * NEV if 1 in directions else 0, 0]
    shapes = [jax.ShapeDtypeStruct((height + extra, 2 * COLS), BF16) for extra in (0, *tall)]
    if leads:
        shapes.append(pltpu.VMEM((3, COLS, SITES), BF16))
    return pl.pallas_call(
        functools.partial(field_kernel, directions),
        out_shape=shapes,
        in_specs=specs,
        out_specs=[VMEM] * len(shapes),
        scratch_shapes=scratch,
        compiler_params=PARAMS,
        cost_estimate=pl.CostEstimate(
            flops=8 * len(directions) * 384 * 768 * 6912, bytes_accessed=6_000_000, transcendentals=0),
        name="field_block",
    )(*args)


def middle_kernel(place, *refs):
    outs, held = refs[11:15], refs[15]
    lead, y, z = refs[:3], refs[3:7], refs[7:11]
    for g in range(4):
        if g < 2:
            rows = slice(g * NEV, g * NEV + NEV)
            terms = [ref[rows, :] for ref in lead] + [y[2][NEV + g * NEV : 2 * NEV + g * NEV, :]]
        else:
            terms = [ref[:NEV, :] for ref in (y, z)[g - 2]]
        summed = terms[0].astype(F32)
        for term in terms[1:]:
            summed = summed + term.astype(F32)
        for owner in range(16):
            held[owner, g * 6 : g * 6 + 6, :] = summed[owner * 6 : owner * 6 + 6, :]
    low = place[1] & 3
    for m in range(4):
        for q in range(4):
            outs[m][q] = held[q * 4 + (low ^ m)].astype(BF16)


def second_kernel(place, own, one, two, three, *outs):
    high = place[1] // 4
    for d in range(4):
        at = (high + d) & 3
        summed = own[at].astype(F32)
        for ref in (one, two, three):
            summed = summed + ref[at].astype(F32)
        outs[d][...] = summed.astype(outs[d].dtype)


def last_kernel(own, one, two, three, order, out):
    below = lax.broadcasted_iota(jnp.int32, (COLS, COLS), 0)
    moves = (below == order[...]).astype(F32).astype(BF16)
    summed = own[...]
    for ref in (one, two, three):
        summed = summed + ref[...].astype(F32)
    for r in range(2):
        rest = summed[:, r * COLS : (r + 1) * COLS]
        moved = None
        for _ in range(3):
            part = rest.astype(BF16)
            rest = rest - part.astype(F32)
            term = dot(part, moves, ((1,), (0,)))
            moved = term if moved is None else moved + term
        for g in range(4):
            out[:, g, r, :] = moved[g * 6 : g * 6 + 6, :]


def call(kernel, shapes, specs, args, name, scratch=()):
    many = isinstance(shapes, list)
    return pl.pallas_call(
        kernel,
        out_shape=shapes,
        in_specs=specs,
        out_specs=[VMEM] * len(shapes) if many else VMEM,
        scratch_shapes=list(scratch),
        compiler_params=PARAMS,
        name=name,
    )(*args)


def prepare(place, momenta, vec, gauge_links, sol):
    shape = jax.ShapeDtypeStruct
    hbm = pltpu.MemorySpace.HBM
    made = call(
        prepare_kernel,
        [
            shape((ROWS, EDGE_Y), BF16),
            shape((ROWS + LINK_ROWS, EDGE_Y), BF16),
            pltpu.VMEM((8, 8, SITES), F32),
            pltpu.VMEM((54, SITES), F32),
            pltpu.VMEM((6, NEV, SITES), BF16),
            pltpu.VMEM((SITES, EDGE_Y), BF16),
            pltpu.VMEM((SITES, EDGE_Y), BF16),
            pltpu.VMEM((6, COLS, SITES), BF16),
        ],
        [SMEM, HBM, HBM, HBM, HBM],
        (
            place,
            pltpu.with_memory_space_constraint(momenta, hbm),
            pltpu.with_memory_space_constraint(vec, hbm),
            pltpu.with_memory_space_constraint(jnp.transpose(gauge_links, (1, 2, 3, 0, 4)), hbm),
            pltpu.with_memory_space_constraint(sol, hbm),
        ),
        "prepare",
        [
            pltpu.SMEM((NMOM, 3), jnp.int32),
            pltpu.VMEM((3, 3, 3, 2, SITES), BF16),
            pltpu.SemaphoreType.DMA((4,)),
        ],
    )
    return [*made[:2], *(in_vmem(a) for a in made[2:])]


def in_vmem(array):
    return pltpu.with_memory_space_constraint(array, pltpu.VMEM)


def body(eigenvectors, gauge_links, solutions, momenta, solution_order):
    vec = eigenvectors.reshape(6, NEV, SITES)
    sol = solutions.reshape(6, COLS, SITES)
    place = jnp.stack((lax.axis_index("gz"), lax.axis_index("gy"))).astype(jnp.int32)
    order = (jnp.tile(solution_order, 4) + (jnp.arange(COLS) // NEV) * NEV).astype(jnp.int32)[None, :]
    y_up, y_down, phase, link, vec, first, last, sol = prepare(place, momenta, vec, gauge_links, sol)
    size = lax.axis_size("gy")
    y_up = lax.ppermute(y_up, "gy", [(i, (i - 1) % size) for i in range(size)])
    y_down = lax.ppermute(y_down, "gy", [(i, (i + 1) % size) for i in range(size)])
    slabs = lax.axis_size("gz")

    def across(block, k):
        return lax.ppermute(block, "gz", [(i, (i + k) % slabs) for i in range(slabs)])

    first_two = field_block((None, 0), place, vec, sol, phase, link, ())
    negated = in_vmem(first_two[4])
    from_below, from_above = across(first_two[1], 1), across(first_two[3], 3)
    along_y = field_block(
        (1,), place, vec, sol, phase, link, (y_up, y_down, first, last, first_two[2], negated))
    parts = [first_two[0], from_below, from_above]
    parts += [along_y[0], across(along_y[1], 1), across(along_y[2], 2), across(along_y[3], 3)]
    along_z = field_block((2,), place, vec, sol, phase, link, (from_above, from_below, negated))
    parts += [along_z[0], across(along_z[1], 1), across(along_z[2], 2), across(along_z[3], 3)]
    shape = jax.ShapeDtypeStruct
    blocks = call(
        middle_kernel,
        [shape((4, 24, 2 * COLS), BF16)] * 4,
        [SMEM] + [VMEM] * 11,
        (place, *parts),
        "middle",
        [pltpu.VMEM((16, 24, 2 * COLS), F32)],
    )
    parts = [blocks[0]]
    for m in range(1, 4):
        parts.append(lax.ppermute(blocks[m], "gy", [(i, i ^ m) for i in range(size)]))
    blocks = call(
        second_kernel,
        [shape((24, 2 * COLS), F32)] + [shape((24, 2 * COLS), BF16)] * 3,
        [SMEM] + [VMEM] * 4,
        (place, *parts),
        "second",
    )
    parts = [blocks[0]]
    for d in range(1, 4):
        parts.append(lax.ppermute(blocks[d], "gy", [(i, (i + 4 * d) % size) for i in range(size)]))
    return call(
        last_kernel,
        shape((6, 4, 2, COLS), F32),
        [VMEM] * 5,
        (*parts, order),
        "last",
    )


def solution(mesh):
    return jax.shard_map(
        body,
        mesh=mesh,
        in_specs=(
            P(None, None, None, ("ta", "gz", "gy")),
            P(None, None, None, None, ("ta", "gz", "gy")),
            P(None, None, None, None, ("ta", "gz", "gy")),
            P(),
            P(),
        ),
        out_specs=P(("ta", "gz", "gy"), None, None, None),
        check_vma=False,
    )
```

```python
import functools

import jax
import jax.numpy as jnp
from jax import lax
from jax.experimental import pallas as pl
from jax.experimental.pallas import tpu as pltpu
from jax.sharding import PartitionSpec as P

NEV = 96
COLS = 384
X = 48
LZ = 48
NY = 48
YD = 3
ZD = 8
PLANE = YD * X
SITES = ZD * PLANE
TILE = 128
TILES = SITES // TILE
NMOM = 4
NZ_DEVICES = 4
EDGE_Y = ZD * X
EDGE_Z = 256
ROWS = 6 * NEV
LINK_ROWS = 32
TWO_PI = 6.283185307179586
F32 = jnp.float32
BF16 = jnp.bfloat16
VMEM = pl.BlockSpec(memory_space=pltpu.VMEM)
SMEM = pl.BlockSpec(memory_space=pltpu.SMEM)
HBM = pl.BlockSpec(memory_space=pltpu.HBM)
PARAMS = pltpu.CompilerParams(vmem_limit_bytes=30 * 1024 * 1024)


def dot(a, b, dims):
    return lax.dot_general(a, b, (dims, ((), ())), preferred_element_type=F32)


def row_site(column, row):
    return column + (column // X) * (PLANE - X) + row * X


def selector(row):
    sites = lax.broadcasted_iota(jnp.int32, (SITES, EDGE_Y), 0)
    column = lax.broadcasted_iota(jnp.int32, (1, EDGE_Y), 1)
    return (sites == row_site(column, row)).astype(F32).astype(BF16)


def periodic(product, size):
    wrapped = product - size * jnp.floor(product / size)
    return jnp.where(wrapped >= size, wrapped - size, wrapped)


def wave(turns):
    quarter = jnp.floor(turns * 4.0 + 0.5)
    angle = (turns - quarter * 0.25) * F32(TWO_PI)
    square = angle * angle
    cosine = 1.0 + square * (-0.5 + square * (1 / 24 + square * (-1 / 720 + square * (1 / 40320))))
    sine = angle * (1.0 + square * (-1 / 6 + square * (1 / 120 + square * (-1 / 5040 + square * (1 / 362880)))))
    quadrant = quarter.astype(jnp.int32) & 3
    odd = (quadrant & 1) == 1
    sign_cosine = jnp.where((quadrant == 1) | (quadrant == 2), -1.0, 1.0)
    sign_sine = jnp.where(quadrant >= 2, -1.0, 1.0)
    return jnp.where(odd, sine, cosine) * sign_cosine, jnp.where(odd, cosine, sine) * sign_sine


def prepare_kernel(
    place, momenta_hbm, vec_hbm, link_hbm, sol_hbm,
    y_up, y_down, phase, flat_link, vec, first_row, last_row, sol,
    momenta, link, sems,
):
    fetches = [
        pltpu.make_async_copy(link_hbm, link, sems.at[0]),
        pltpu.make_async_copy(momenta_hbm, momenta, sems.at[1]),
        pltpu.make_async_copy(vec_hbm, vec, sems.at[2]),
        pltpu.make_async_copy(sol_hbm, sol, sems.at[3]),
    ]
    for fetch in fetches:
        fetch.start()
    first_row[...] = selector(0)
    last_row[...] = selector(YD - 1)
    first, last = first_row[...], last_row[...]
    fetches[0].wait()
    for q in range(27):
        flat_link[2 * q : 2 * q + 2, :] = link[q // 9, (q // 3) % 3, q % 3].astype(F32)
    pad = jnp.zeros((LINK_ROWS - 18, SITES), F32)
    y_link = jnp.concatenate((flat_link[18:36, :], pad), axis=0).astype(BF16)
    y_down[ROWS:, :] = dot(y_link, last, ((1,), (0,))).astype(BF16)
    fetches[1].wait()
    sites = lax.broadcasted_iota(jnp.int32, (8, SITES), 1)
    row = lax.broadcasted_iota(jnp.int32, (8, SITES), 0)
    slab = sites // PLANE
    within = sites - slab * PLANE
    line = within // X
    column = (within - line * X).astype(F32)
    slab = (slab + place[0] * ZD).astype(F32)
    line = (line + place[1] * YD).astype(F32)
    along = [jnp.zeros((8, SITES), F32) for _ in range(3)]
    for p in range(NMOM):
        for axis in range(3):
            value = momenta[(place[0] + p) & 3, axis].astype(F32)
            along[axis] = jnp.where((row & 3) == p, value, along[axis])
    x_part = periodic(along[0] * column, float(X)) / X
    y_part = periodic(along[1] * line, float(NY)) / NY
    z_part = periodic(along[2] * slab, float(LZ)) / LZ
    cosine, sine = wave(x_part + y_part + z_part)
    table = jnp.where(row < 4, cosine, sine)
    for k in range(8):
        phase[k] = jnp.broadcast_to(table[k : k + 1, :], (8, SITES))
    fetches[2].wait()
    flat = vec[...].reshape(ROWS, SITES)
    y_up[...] = dot(flat, first, ((1,), (0,))).astype(BF16)
    y_down[:ROWS, :] = dot(flat, last, ((1,), (0,))).astype(BF16)
    fetches[3].wait()


def choose(mask, yes, no):
    parts = (yes.shape[0] // 8, 8, SITES)
    return jnp.where(mask[None], yes.reshape(parts), no.reshape(parts)).reshape(yes.shape)


def shift_x(block, step):
    x = lax.broadcasted_iota(jnp.int32, (8, SITES), 1) % X
    near = pltpu.roll(block, (-step) % SITES, 1)
    far = pltpu.roll(block, (step * (X - 1)) % SITES, 1)
    return choose(x == (X - 1 if step > 0 else 0), far, near)


def shift_y(block, far, step):
    line = (lax.broadcasted_iota(jnp.int32, (8, SITES), 1) // X) % YD
    near = pltpu.roll(block, (-step * X) % SITES, 1)
    return choose(line == (YD - 1 if step > 0 else 0), far, near)


def shift_z(block, halo, step):
    wide = SITES + EDGE_Z
    if step > 0:
        joined = jnp.concatenate((block, halo), axis=1)
        return pltpu.roll(joined, wide - PLANE, 1)[:, :SITES]
    joined = jnp.concatenate((halo, block), axis=1)
    return pltpu.roll(joined, wide - (EDGE_Z - PLANE), 1)[:, :SITES]


def weigh(field, cosine, sine):
    real, imag = field
    return cosine * real - sine * imag, cosine * imag + sine * real


def rounded(block):
    return block.reshape(16, TILE).astype(BF16).astype(F32).reshape(2, 8, TILE)


def field_tile(direction, vec, ahead, behind, wide, rows, lanes):
    def tile(ref, block):
        return ref[block, rows, lanes].astype(F32).reshape(2, 8, TILE)

    if direction is None:
        return [(tile(vec, c), tile(vec, 3 + c)) for c in range(3)]
    forward = [(tile(ahead, c), tile(ahead, 3 + c)) for c in range(3)]
    back = [(tile(behind, c), tile(behind, 3 + c)) for c in range(3)]
    fields = []
    for a in range(3):
        real = imag = low_real = low_imag = None
        for b in range(3):
            ahead_at, behind_at = 2 * (a * 3 + b), 18 + 2 * (b * 3 + a)
            ur, ui = wide[ahead_at, :, lanes], wide[ahead_at + 1, :, lanes]
            dr, di = wide[behind_at, :, lanes], wide[behind_at + 1, :, lanes]
            vr, vi = forward[b]
            br, bi = back[b]
            terms = (ur * vr - ui * vi, ur * vi + ui * vr, dr * br + di * bi, dr * bi - di * br)
            if b == 0:
                real, imag, low_real, low_imag = terms
            else:
                real, imag, low_real, low_imag = (
                    real + terms[0], imag + terms[1], low_real + terms[2], low_imag + terms[3])
        fields.append((real - rounded(low_real), imag - rounded(low_imag)))
    return fields


def shift_all(direction, place, vec, link, halo, ahead, behind, wide):
    links = link[18 * direction : 18 * direction + 18, :]
    links = jnp.concatenate((links, jnp.zeros((14, SITES), F32)), axis=0)
    if direction == 1:
        from_above = dot(halo[0][...], halo[3][...], ((1,), (1,)))
        ahead[...] = from_above.astype(BF16).reshape(6, NEV, SITES)
        from_below = dot(halo[1][...], halo[2][...], ((1,), (1,)))
        behind[...] = from_below[:ROWS, :].astype(BF16).reshape(6, NEV, SITES)
    if direction == 2:
        keep_up = (place[0] < NZ_DEVICES - 1).astype(F32)
        keep_down = (place[0] > 0).astype(F32)
    for block in range(6):
        here = vec[block].astype(F32)
        rows = pl.ds(block * NEV, NEV)
        if direction == 0:
            front, rear = shift_x(here, 1), shift_x(here, -1)
        elif direction == 1:
            front = shift_y(here, ahead[block].astype(F32), 1)
            rear = shift_y(here, behind[block].astype(F32), -1)
        else:
            rows = slice(2 * NEV + block % 2 * NEV, 3 * NEV + block % 2 * NEV)
            columns = slice(block // 2 * EDGE_Z, block // 2 * EDGE_Z + EDGE_Z)
            front = shift_z(here, halo[0][rows, columns].astype(F32) * keep_up, 1)
            rear = shift_z(here, halo[1][rows, columns].astype(F32) * keep_down, -1)
        ahead[block] = front.astype(BF16)
        behind[block] = rear.astype(BF16)
    if direction == 0:
        links_below = shift_x(links, -1)
    elif direction == 1:
        links_below = shift_y(links, from_below[ROWS:, :], -1)
    else:
        links_below = shift_z(links, halo[1][4 * NEV :, :EDGE_Z].astype(F32) * keep_down, -1)
    for k in range(18):
        wide[k] = jnp.broadcast_to(links[k : k + 1, :], (8, SITES))
        wide[18 + k] = jnp.broadcast_to(links_below[k : k + 1, :], (8, SITES))


def field_kernel(directions, *refs):
    refs = list(refs)
    place, vec, sol, phase, link = [refs.pop(0) for _ in range(5)]
    halos = [[refs.pop(0) for _ in range(HALOS[d])] for d in directions]
    outs = [refs.pop(0) for _ in range(NMOM)]
    height = NEV * len(directions)
    leads = directions[0] is None
    if leads:
        negated = refs.pop(0)
    else:
        negated = halos[-1].pop()
    if 1 in directions:
        outs[2][NEV:, :] = halos[0].pop()[...]
    weighted = [refs.pop(0), refs.pop(0)]
    total = refs.pop(0)
    shifted = [[refs.pop(0) for _ in range(0 if d is None else 3)] for d in directions]
    for d, halo, kept in zip(directions, halos, shifted):
        if d is not None:
            shift_all(d, place, vec, link, halo, *kept)

    def fill(tile, slot, part):
        lanes = pl.ds(tile * TILE if isinstance(tile, int) else pl.multiple_of(tile * TILE, TILE), TILE)
        for e in range(2 * part, 2 * part + 2):
            for f, d in enumerate(directions):
                ahead, behind, wide = shifted[f] if shifted[f] else (None, None, None)
                fields = field_tile(d, vec, ahead, behind, wide, pl.ds(e * 16, 16), lanes)
                for p in range(NMOM):
                    cosine, sine = phase[p, :, lanes], phase[4 + p, :, lanes]
                    rows = pl.ds((p * len(directions) + f) * NEV + e * 16, 16)
                    for c in range(3):
                        real, imag = weigh(fields[c], cosine, sine)
                        weighted[slot][rows, c * TILE : (c + 1) * TILE] = real.reshape(16, TILE).astype(BF16)
                        weighted[slot][rows, (3 + c) * TILE : (4 + c) * TILE] = imag.reshape(16, TILE).astype(BF16)

    def right_hand(lanes, k, first, stop):
        pieces = []
        if first < COLS:
            pieces.append(sol[k, first : min(stop, COLS), lanes])
        if stop > COLS:
            rows = slice(max(first, COLS) - COLS, stop - COLS)
            pieces.append(sol[3 + k, rows, lanes] if k < 3 else negated[k - 3, rows, lanes])
        return pieces[0] if len(pieces) == 1 else jnp.concatenate(pieces, axis=0)

    def multiply(tile, slot, part):
        lanes = pl.ds(tile * TILE if isinstance(tile, int) else pl.multiple_of(tile * TILE, TILE), TILE)
        columns = pl.ds(part * 256, 256)
        right = jnp.concatenate([right_hand(lanes, k, part * 256, part * 256 + 256) for k in range(6)], axis=1)
        product = dot(weighted[slot][...], right, ((1,), (1,)))
        total[:, columns] = total[:, columns] + product

    for part in range(3):
        fill(0, 0, part)
    if leads:
        for c in range(3):
            negated[c] = -sol[c]
        for third in range(3):
            columns = slice(third * EDGE_Z, third * EDGE_Z + EDGE_Z)
            for b in range(2):
                at = slice(height + b * NEV, height + b * NEV + NEV)
                outs[3][at, columns] = vec[2 * third + b, :, :EDGE_Z]
                outs[1][at, columns] = vec[2 * third + b, :, SITES - EDGE_Z :]
        z_link = jnp.concatenate((link[36:54, SITES - EDGE_Z :], jnp.zeros((LINK_ROWS - 18, EDGE_Z), F32)), axis=0)
        outs[1][height + 2 * NEV :, :EDGE_Z] = z_link.astype(BF16)
        outs[1][height + 2 * NEV :, EDGE_Z:] = jnp.zeros((LINK_ROWS, 2 * EDGE_Z), BF16)
    total[...] = jnp.zeros_like(total)

    def step(i, carry):
        for tile, slot in ((4 * i, 0), (4 * i + 1, 1), (4 * i + 2, 0), (4 * i + 3, 1)):
            for part in range(3):
                multiply(tile, slot, part)
                fill(tile + 1, 1 - slot, part)
        return carry

    lax.fori_loop(0, TILES // 4, step, 0)
    for part in range(3):
        multiply(TILES - 1, 0, part)
    for p in range(NMOM):
        outs[p][:height, :] = total[p * height : (p + 1) * height, :].astype(BF16)


HALOS = {None: 0, 0: 0, 1: 6, 2: 3}


def field_block(directions, place, vec, sol, phase, link, halos):
    height = NEV * len(directions)
    leads = directions[0] is None
    scratch = [
        pltpu.VMEM((NMOM * height, 6 * TILE), BF16),
        pltpu.VMEM((NMOM * height, 6 * TILE), BF16),
        pltpu.VMEM((NMOM * height, 2 * COLS), F32),
    ]
    args = [place, vec, sol, phase, link, *halos]
    specs = [SMEM] + [VMEM] * (len(args) - 1)
    for d in directions:
        if d is not None:
            scratch += [pltpu.VMEM((6, NEV, SITES), BF16)] * 2 + [pltpu.VMEM((36, 8, SITES), F32)]
    tall = [2 * NEV + LINK_ROWS, 0, 2 * NEV] if leads else [0, 2 * NEV if 1 in directions else 0, 0]
    shapes = [jax.ShapeDtypeStruct((height + extra, 2 * COLS), BF16) for extra in (0, *tall)]
    if leads:
        shapes.append(pltpu.VMEM((3, COLS, SITES), BF16))
    return pl.pallas_call(
        functools.partial(field_kernel, directions),
        out_shape=shapes,
        in_specs=specs,
        out_specs=[VMEM] * len(shapes),
        scratch_shapes=scratch,
        compiler_params=PARAMS,
        cost_estimate=pl.CostEstimate(
            flops=8 * len(directions) * 384 * 768 * 6912, bytes_accessed=6_000_000, transcendentals=0),
        name="field_block",
    )(*args)


def middle_kernel(place, *refs):
    outs, held = refs[11:15], refs[15]
    lead, y, z = refs[:3], refs[3:7], refs[7:11]
    for g in range(4):
        if g < 2:
            rows = slice(g * NEV, g * NEV + NEV)
            terms = [ref[rows, :] for ref in lead] + [y[2][NEV + g * NEV : 2 * NEV + g * NEV, :]]
        else:
            terms = [ref[:NEV, :] for ref in (y, z)[g - 2]]
        summed = terms[0].astype(F32)
        for term in terms[1:]:
            summed = summed + term.astype(F32)
        for owner in range(16):
            held[owner, g * 6 : g * 6 + 6, :] = summed[owner * 6 : owner * 6 + 6, :]
    low = place[1] & 3
    for m in range(4):
        for q in range(4):
            outs[m][q] = held[q * 4 + (low ^ m)].astype(BF16)


def second_kernel(place, own, one, two, three, *outs):
    high = place[1] // 4
    for d in range(4):
        at = (high + d) & 3
        summed = own[at].astype(F32)
        for ref in (one, two, three):
            summed = summed + ref[at].astype(F32)
        outs[d][...] = summed.astype(outs[d].dtype)


def last_kernel(own, one, two, three, order, out):
    below = lax.broadcasted_iota(jnp.int32, (COLS, COLS), 0)
    moves = (below == order[...]).astype(F32).astype(BF16)
    summed = own[...]
    for ref in (one, two, three):
        summed = summed + ref[...].astype(F32)
    for r in range(2):
        rest = summed[:, r * COLS : (r + 1) * COLS]
        moved = None
        for _ in range(3):
            part = rest.astype(BF16)
            rest = rest - part.astype(F32)
            term = dot(part, moves, ((1,), (0,)))
            moved = term if moved is None else moved + term
        for g in range(4):
            out[:, g, r, :] = moved[g * 6 : g * 6 + 6, :]


def call(kernel, shapes, specs, args, name, scratch=()):
    many = isinstance(shapes, list)
    return pl.pallas_call(
        kernel,
        out_shape=shapes,
        in_specs=specs,
        out_specs=[VMEM] * len(shapes) if many else VMEM,
        scratch_shapes=list(scratch),
        compiler_params=PARAMS,
        name=name,
    )(*args)


def prepare(place, momenta, vec, gauge_links, sol):
    shape = jax.ShapeDtypeStruct
    hbm = pltpu.MemorySpace.HBM
    made = call(
        prepare_kernel,
        [
            shape((ROWS, EDGE_Y), BF16),
            shape((ROWS + LINK_ROWS, EDGE_Y), BF16),
            pltpu.VMEM((8, 8, SITES), F32),
            pltpu.VMEM((54, SITES), F32),
            pltpu.VMEM((6, NEV, SITES), BF16),
            pltpu.VMEM((SITES, EDGE_Y), BF16),
            pltpu.VMEM((SITES, EDGE_Y), BF16),
            pltpu.VMEM((6, COLS, SITES), BF16),
        ],
        [SMEM, HBM, HBM, HBM, HBM],
        (
            place,
            pltpu.with_memory_space_constraint(momenta, hbm),
            pltpu.with_memory_space_constraint(vec, hbm),
            pltpu.with_memory_space_constraint(jnp.transpose(gauge_links, (1, 2, 3, 0, 4)), hbm),
            pltpu.with_memory_space_constraint(sol, hbm),
        ),
        "prepare",
        [
            pltpu.SMEM((NMOM, 3), jnp.int32),
            pltpu.VMEM((3, 3, 3, 2, SITES), BF16),
            pltpu.SemaphoreType.DMA((4,)),
        ],
    )
    return [*made[:2], *(in_vmem(a) for a in made[2:])]


def in_vmem(array):
    return pltpu.with_memory_space_constraint(array, pltpu.VMEM)


def body(eigenvectors, gauge_links, solutions, momenta, solution_order):
    vec = eigenvectors.reshape(6, NEV, SITES)
    sol = solutions.reshape(6, COLS, SITES)
    place = jnp.stack((lax.axis_index("gz"), lax.axis_index("gy"))).astype(jnp.int32)
    order = (jnp.tile(solution_order, 4) + (jnp.arange(COLS) // NEV) * NEV).astype(jnp.int32)[None, :]
    y_up, y_down, phase, link, vec, first, last, sol = prepare(place, momenta, vec, gauge_links, sol)
    size = lax.axis_size("gy")
    y_up = lax.ppermute(y_up, "gy", [(i, (i - 1) % size) for i in range(size)])
    y_down = lax.ppermute(y_down, "gy", [(i, (i + 1) % size) for i in range(size)])
    slabs = lax.axis_size("gz")

    def across(block, k):
        return lax.ppermute(block, "gz", [(i, (i + k) % slabs) for i in range(slabs)])

    first_two = field_block((None, 0), place, vec, sol, phase, link, ())
    negated = in_vmem(first_two[4])
    from_below, from_above = across(first_two[1], 1), across(first_two[3], 3)
    along_y = field_block(
        (1,), place, vec, sol, phase, link, (y_up, y_down, first, last, first_two[2], negated))
    parts = [first_two[0], from_below, from_above]
    parts += [along_y[0], across(along_y[1], 1), across(along_y[2], 2), across(along_y[3], 3)]
    along_z = field_block((2,), place, vec, sol, phase, link, (from_above, from_below, negated))
    parts += [along_z[0], across(along_z[1], 1), across(along_z[2], 2), across(along_z[3], 3)]
    shape = jax.ShapeDtypeStruct
    blocks = call(
        middle_kernel,
        [shape((4, 24, 2 * COLS), BF16)] * 4,
        [SMEM] + [VMEM] * 11,
        (place, *parts),
        "middle",
        [pltpu.VMEM((16, 24, 2 * COLS), F32)],
    )
    parts = [blocks[0]]
    for m in range(1, 4):
        parts.append(lax.ppermute(blocks[m], "gy", [(i, i ^ m) for i in range(size)]))
    blocks = call(
        second_kernel,
        [shape((24, 2 * COLS), F32)] + [shape((24, 2 * COLS), BF16)] * 3,
        [SMEM] + [VMEM] * 4,
        (place, *parts),
        "second",
    )
    parts = [blocks[0]]
    for d in range(1, 4):
        parts.append(lax.ppermute(blocks[d], "gy", [(i, (i + 4 * d) % size) for i in range(size)]))
    return call(
        last_kernel,
        shape((6, 4, 2, COLS), F32),
        [VMEM] * 5,
        (*parts, order),
        "last",
    )


def solution(mesh):
    return jax.shard_map(
        body,
        mesh=mesh,
        in_specs=(
            P(None, None, None, ("ta", "gz", "gy")),
            P(None, None, None, None, ("ta", "gz", "gy")),
            P(None, None, None, None, ("ta", "gz", "gy")),
            P(),
            P(),
        ),
        out_specs=P(("ta", "gz", "gy"), None, None, None),
        check_vma=False,
    )
```

```python
import functools

import jax
import jax.numpy as jnp
from jax import lax
from jax.experimental import pallas as pl
from jax.experimental.pallas import tpu as pltpu
from jax.sharding import PartitionSpec as P

NEV = 96
COLS = 384
X = 48
LZ = 48
NY = 48
YD = 3
ZD = 8
PLANE = YD * X
SITES = ZD * PLANE
TILE = 128
TILES = SITES // TILE
NMOM = 4
NZ_DEVICES = 4
EDGE_Y = ZD * X
EDGE_Z = 256
ROWS = 6 * NEV
LINK_ROWS = 32
TWO_PI = 6.283185307179586
F32 = jnp.float32
BF16 = jnp.bfloat16
VMEM = pl.BlockSpec(memory_space=pltpu.VMEM)
SMEM = pl.BlockSpec(memory_space=pltpu.SMEM)
HBM = pl.BlockSpec(memory_space=pltpu.HBM)
PARAMS = pltpu.CompilerParams(vmem_limit_bytes=30 * 1024 * 1024)


def dot(a, b, dims):
    return lax.dot_general(a, b, (dims, ((), ())), preferred_element_type=F32)


def row_site(column, row):
    return column + (column // X) * (PLANE - X) + row * X


def selector(row):
    sites = lax.broadcasted_iota(jnp.int32, (SITES, EDGE_Y), 0)
    column = lax.broadcasted_iota(jnp.int32, (1, EDGE_Y), 1)
    return (sites == row_site(column, row)).astype(F32).astype(BF16)


def periodic(product, size):
    wrapped = product - size * jnp.floor(product / size)
    return jnp.where(wrapped >= size, wrapped - size, wrapped)


def wave(turns):
    quarter = jnp.floor(turns * 4.0 + 0.5)
    angle = (turns - quarter * 0.25) * F32(TWO_PI)
    square = angle * angle
    cosine = 1.0 + square * (-0.5 + square * (1 / 24 + square * (-1 / 720 + square * (1 / 40320))))
    sine = angle * (1.0 + square * (-1 / 6 + square * (1 / 120 + square * (-1 / 5040 + square * (1 / 362880)))))
    quadrant = quarter.astype(jnp.int32) & 3
    odd = (quadrant & 1) == 1
    sign_cosine = jnp.where((quadrant == 1) | (quadrant == 2), -1.0, 1.0)
    sign_sine = jnp.where(quadrant >= 2, -1.0, 1.0)
    return jnp.where(odd, sine, cosine) * sign_cosine, jnp.where(odd, cosine, sine) * sign_sine


def prepare_kernel(
    place, momenta_hbm, vec_hbm, link_hbm, sol_hbm,
    y_up, y_down, phase, flat_link, vec, edges, sol,
    momenta, link, sems,
):
    fetches = [
        pltpu.make_async_copy(link_hbm, link, sems.at[0]),
        pltpu.make_async_copy(momenta_hbm, momenta, sems.at[1]),
        pltpu.make_async_copy(vec_hbm, vec, sems.at[2]),
        pltpu.make_async_copy(sol_hbm, sol, sems.at[3]),
    ]
    for fetch in fetches:
        fetch.start()
    edges[:, :EDGE_Y] = selector(0)
    edges[:, EDGE_Y:] = selector(YD - 1)
    fetches[0].wait()
    for q in range(27):
        flat_link[2 * q : 2 * q + 2, :] = link[q // 9, (q // 3) % 3, q % 3].astype(F32)
    pad = jnp.zeros((LINK_ROWS - 18, SITES), F32)
    y_link = jnp.concatenate((flat_link[18:36, :], pad), axis=0).astype(BF16)
    fetches[1].wait()
    sites = lax.broadcasted_iota(jnp.int32, (8, SITES), 1)
    row = lax.broadcasted_iota(jnp.int32, (8, SITES), 0)
    slab = sites // PLANE
    within = sites - slab * PLANE
    line = within // X
    column = (within - line * X).astype(F32)
    slab = (slab + place[0] * ZD).astype(F32)
    line = (line + place[1] * YD).astype(F32)
    along = [jnp.zeros((8, SITES), F32) for _ in range(3)]
    for p in range(NMOM):
        for axis in range(3):
            value = momenta[(place[0] + p) & 3, axis].astype(F32)
            along[axis] = jnp.where((row & 3) == p, value, along[axis])
    x_part = periodic(along[0] * column, float(X)) / X
    y_part = periodic(along[1] * line, float(NY)) / NY
    z_part = periodic(along[2] * slab, float(LZ)) / LZ
    cosine, sine = wave(x_part + y_part + z_part)
    table = jnp.where(row < 4, cosine, sine)
    for k in range(8):
        phase[k] = jnp.broadcast_to(table[k : k + 1, :], (8, SITES))
    fetches[2].wait()
    flat = jnp.concatenate((vec[...].reshape(ROWS, SITES), y_link), axis=0)
    compact = dot(flat, edges[...], ((1,), (0,))).astype(BF16)
    y_up[...] = compact[:ROWS, :EDGE_Y]
    y_down[...] = compact[:, EDGE_Y:]
    fetches[3].wait()


def choose(mask, yes, no):
    parts = (yes.shape[0] // 8, 8, SITES)
    return jnp.where(mask[None], yes.reshape(parts), no.reshape(parts)).reshape(yes.shape)


def shift_x(block, step):
    x = lax.broadcasted_iota(jnp.int32, (8, SITES), 1) % X
    near = pltpu.roll(block, (-step) % SITES, 1)
    far = pltpu.roll(block, (step * (X - 1)) % SITES, 1)
    return choose(x == (X - 1 if step > 0 else 0), far, near)


def shift_y(block, far, step):
    line = (lax.broadcasted_iota(jnp.int32, (8, SITES), 1) // X) % YD
    near = pltpu.roll(block, (-step * X) % SITES, 1)
    return choose(line == (YD - 1 if step > 0 else 0), far, near)


def shift_z(block, halo, step):
    wide = SITES + EDGE_Z
    if step > 0:
        joined = jnp.concatenate((block, halo), axis=1)
        return pltpu.roll(joined, wide - PLANE, 1)[:, :SITES]
    joined = jnp.concatenate((halo, block), axis=1)
    return pltpu.roll(joined, wide - (EDGE_Z - PLANE), 1)[:, :SITES]


def weigh(field, cosine, sine):
    real, imag = field
    return cosine * real - sine * imag, cosine * imag + sine * real


def rounded(block):
    return block.reshape(16, TILE).astype(BF16).astype(F32).reshape(2, 8, TILE)


def field_tile(direction, vec, ahead, behind, wide, rows, lanes):
    def tile(ref, block):
        return ref[block, rows, lanes].astype(F32).reshape(2, 8, TILE)

    if direction is None:
        return [(tile(vec, c), tile(vec, 3 + c)) for c in range(3)]
    forward = [(tile(ahead, c), tile(ahead, 3 + c)) for c in range(3)]
    back = [(tile(behind, c), tile(behind, 3 + c)) for c in range(3)]
    fields = []
    for a in range(3):
        real = imag = low_real = low_imag = None
        for b in range(3):
            ahead_at, behind_at = 2 * (a * 3 + b), 18 + 2 * (b * 3 + a)
            ur, ui = wide[ahead_at, :, lanes], wide[ahead_at + 1, :, lanes]
            dr, di = wide[behind_at, :, lanes], wide[behind_at + 1, :, lanes]
            vr, vi = forward[b]
            br, bi = back[b]
            terms = (ur * vr - ui * vi, ur * vi + ui * vr, dr * br + di * bi, dr * bi - di * br)
            if b == 0:
                real, imag, low_real, low_imag = terms
            else:
                real, imag, low_real, low_imag = (
                    real + terms[0], imag + terms[1], low_real + terms[2], low_imag + terms[3])
        fields.append((real - rounded(low_real), imag - rounded(low_imag)))
    return fields


def shift_all(direction, place, vec, link, halo, ahead, behind, wide):
    links = link[18 * direction : 18 * direction + 18, :]
    links = jnp.concatenate((links, jnp.zeros((14, SITES), F32)), axis=0)
    if direction == 1:
        above = jnp.concatenate((halo[0][...], jnp.zeros((LINK_ROWS, EDGE_Y), BF16)), axis=0)
        far = dot(jnp.concatenate((halo[1][...], above), axis=1), halo[2][...], ((1,), (1,)))
        ahead[...] = far[:ROWS, :].astype(BF16).reshape(6, NEV, SITES)
    if direction == 2:
        keep_up = (place[0] < NZ_DEVICES - 1).astype(F32)
        keep_down = (place[0] > 0).astype(F32)
    for block in range(6):
        here = vec[block].astype(F32)
        rows = pl.ds(block * NEV, NEV)
        if direction == 0:
            front, rear = shift_x(here, 1), shift_x(here, -1)
        elif direction == 1:
            from_devices = ahead[block].astype(F32)
            front = shift_y(here, from_devices, 1)
            rear = shift_y(here, from_devices, -1)
        else:
            rows = slice(2 * NEV + block % 2 * NEV, 3 * NEV + block % 2 * NEV)
            columns = slice(block // 2 * EDGE_Z, block // 2 * EDGE_Z + EDGE_Z)
            front = shift_z(here, halo[0][rows, columns].astype(F32) * keep_up, 1)
            rear = shift_z(here, halo[1][rows, columns].astype(F32) * keep_down, -1)
        ahead[block] = front.astype(BF16)
        behind[block] = rear.astype(BF16)
    if direction == 0:
        links_below = shift_x(links, -1)
    elif direction == 1:
        links_below = shift_y(links, far[ROWS:, :], -1)
    else:
        links_below = shift_z(links, halo[1][4 * NEV :, :EDGE_Z].astype(F32) * keep_down, -1)
    for k in range(18):
        wide[k] = jnp.broadcast_to(links[k : k + 1, :], (8, SITES))
        wide[18 + k] = jnp.broadcast_to(links_below[k : k + 1, :], (8, SITES))


def field_kernel(directions, *refs):
    refs = list(refs)
    place, vec, sol, phase, link = [refs.pop(0) for _ in range(5)]
    halos = [[refs.pop(0) for _ in range(HALOS[d])] for d in directions]
    outs = [refs.pop(0) for _ in range(NMOM)]
    height = NEV * len(directions)
    leads = directions[0] is None
    if leads:
        negated = refs.pop(0)
    else:
        negated = halos[-1].pop()
    if 1 in directions:
        outs[2][NEV:, :] = halos[0].pop()[...]
    weighted = [refs.pop(0), refs.pop(0)]
    total = refs.pop(0)
    shifted = [[refs.pop(0) for _ in range(0 if d is None else 3)] for d in directions]
    for d, halo, kept in zip(directions, halos, shifted):
        if d is not None:
            shift_all(d, place, vec, link, halo, *kept)

    def fill(tile, slot, part):
        lanes = pl.ds(tile * TILE if isinstance(tile, int) else pl.multiple_of(tile * TILE, TILE), TILE)
        for e in range(2 * part, 2 * part + 2):
            for f, d in enumerate(directions):
                ahead, behind, wide = shifted[f] if shifted[f] else (None, None, None)
                fields = field_tile(d, vec, ahead, behind, wide, pl.ds(e * 16, 16), lanes)
                for p in range(NMOM):
                    cosine, sine = phase[p, :, lanes], phase[4 + p, :, lanes]
                    rows = pl.ds((p * len(directions) + f) * NEV + e * 16, 16)
                    for c in range(3):
                        real, imag = weigh(fields[c], cosine, sine)
                        weighted[slot][rows, c * TILE : (c + 1) * TILE] = real.reshape(16, TILE).astype(BF16)
                        weighted[slot][rows, (3 + c) * TILE : (4 + c) * TILE] = imag.reshape(16, TILE).astype(BF16)

    def right_hand(lanes, k, first, stop):
        pieces = []
        if first < COLS:
            pieces.append(sol[k, first : min(stop, COLS), lanes])
        if stop > COLS:
            rows = slice(max(first, COLS) - COLS, stop - COLS)
            pieces.append(sol[3 + k, rows, lanes] if k < 3 else negated[k - 3, rows, lanes])
        return pieces[0] if len(pieces) == 1 else jnp.concatenate(pieces, axis=0)

    def multiply(tile, slot, part):
        lanes = pl.ds(tile * TILE if isinstance(tile, int) else pl.multiple_of(tile * TILE, TILE), TILE)
        columns = pl.ds(part * 256, 256)
        right = jnp.concatenate([right_hand(lanes, k, part * 256, part * 256 + 256) for k in range(6)], axis=1)
        product = dot(weighted[slot][...], right, ((1,), (1,)))
        total[:, columns] = total[:, columns] + product

    for part in range(3):
        fill(0, 0, part)
    if leads:
        for c in range(3):
            negated[c] = -sol[c]
        for third in range(3):
            columns = slice(third * EDGE_Z, third * EDGE_Z + EDGE_Z)
            for b in range(2):
                at = slice(height + b * NEV, height + b * NEV + NEV)
                outs[3][at, columns] = vec[2 * third + b, :, :EDGE_Z]
                outs[1][at, columns] = vec[2 * third + b, :, SITES - EDGE_Z :]
        z_link = jnp.concatenate((link[36:54, SITES - EDGE_Z :], jnp.zeros((LINK_ROWS - 18, EDGE_Z), F32)), axis=0)
        outs[1][height + 2 * NEV :, :EDGE_Z] = z_link.astype(BF16)
        outs[1][height + 2 * NEV :, EDGE_Z:] = jnp.zeros((LINK_ROWS, 2 * EDGE_Z), BF16)
    total[...] = jnp.zeros_like(total)

    def step(i, carry):
        for tile, slot in ((4 * i, 0), (4 * i + 1, 1), (4 * i + 2, 0), (4 * i + 3, 1)):
            for part in range(3):
                multiply(tile, slot, part)
                fill(tile + 1, 1 - slot, part)
        return carry

    lax.fori_loop(0, TILES // 4, step, 0)
    for part in range(3):
        multiply(TILES - 1, 0, part)
    for p in range(NMOM):
        outs[p][:height, :] = total[p * height : (p + 1) * height, :].astype(BF16)


HALOS = {None: 0, 0: 0, 1: 5, 2: 3}


def field_block(directions, place, vec, sol, phase, link, halos):
    height = NEV * len(directions)
    leads = directions[0] is None
    scratch = [
        pltpu.VMEM((NMOM * height, 6 * TILE), BF16),
        pltpu.VMEM((NMOM * height, 6 * TILE), BF16),
        pltpu.VMEM((NMOM * height, 2 * COLS), F32),
    ]
    args = [place, vec, sol, phase, link, *halos]
    specs = [SMEM] + [VMEM] * (len(args) - 1)
    for d in directions:
        if d is not None:
            scratch += [pltpu.VMEM((6, NEV, SITES), BF16)] * 2 + [pltpu.VMEM((36, 8, SITES), F32)]
    tall = [2 * NEV + LINK_ROWS, 0, 2 * NEV] if leads else [0, 2 * NEV if 1 in directions else 0, 0]
    shapes = [jax.ShapeDtypeStruct((height + extra, 2 * COLS), BF16) for extra in (0, *tall)]
    if leads:
        shapes.append(pltpu.VMEM((3, COLS, SITES), BF16))
    return pl.pallas_call(
        functools.partial(field_kernel, directions),
        out_shape=shapes,
        in_specs=specs,
        out_specs=[VMEM] * len(shapes),
        scratch_shapes=scratch,
        compiler_params=PARAMS,
        cost_estimate=pl.CostEstimate(
            flops=8 * len(directions) * 384 * 768 * 6912, bytes_accessed=6_000_000, transcendentals=0),
        name="field_block",
    )(*args)


def total_of(terms):
    summed = terms[0].astype(F32)
    for term in terms[1:]:
        summed = summed + term.astype(F32)
    return summed


def early_kernel(*refs):
    lead, y, out = refs[:3], refs[3:7], refs[7]
    for g in range(2):
        rows = slice(g * NEV, g * NEV + NEV)
        out[g] = total_of([ref[rows, :] for ref in lead] + [y[2][NEV + g * NEV : 2 * NEV + g * NEV, :]])
    out[2] = total_of([ref[:NEV, :] for ref in y])


def middle_kernel(place, early, *refs):
    outs, held = refs[4:8], refs[8]
    for g in range(4):
        summed = early[g] if g < 3 else total_of([ref[...] for ref in refs[:4]])
        for owner in range(16):
            held[owner, g * 6 : g * 6 + 6, :] = summed[owner * 6 : owner * 6 + 6, :]
    low = place[1] & 3
    for m in range(4):
        for q in range(4):
            outs[m][q] = held[q * 4 + (low ^ m)].astype(BF16)


def second_kernel(place, own, one, two, three, *outs):
    high = place[1] // 4
    for d in range(4):
        at = (high + d) & 3
        summed = own[at].astype(F32)
        for ref in (one, two, three):
            summed = summed + ref[at].astype(F32)
        outs[d][...] = summed.astype(outs[d].dtype)


def last_kernel(own, one, two, three, order, out):
    below = lax.broadcasted_iota(jnp.int32, (COLS, COLS), 0)
    moves = (below == order[...]).astype(F32).astype(BF16)
    summed = own[...]
    for ref in (one, two, three):
        summed = summed + ref[...].astype(F32)
    for r in range(2):
        rest = summed[:, r * COLS : (r + 1) * COLS]
        moved = None
        for _ in range(3):
            part = rest.astype(BF16)
            rest = rest - part.astype(F32)
            term = dot(part, moves, ((1,), (0,)))
            moved = term if moved is None else moved + term
        for g in range(4):
            out[:, g, r, :] = moved[g * 6 : g * 6 + 6, :]


def call(kernel, shapes, specs, args, name, scratch=()):
    many = isinstance(shapes, list)
    return pl.pallas_call(
        kernel,
        out_shape=shapes,
        in_specs=specs,
        out_specs=[VMEM] * len(shapes) if many else VMEM,
        scratch_shapes=list(scratch),
        compiler_params=PARAMS,
        name=name,
    )(*args)


def prepare(place, momenta, vec, gauge_links, sol):
    shape = jax.ShapeDtypeStruct
    hbm = pltpu.MemorySpace.HBM
    made = call(
        prepare_kernel,
        [
            shape((ROWS, EDGE_Y), BF16),
            shape((ROWS + LINK_ROWS, EDGE_Y), BF16),
            pltpu.VMEM((8, 8, SITES), F32),
            pltpu.VMEM((54, SITES), F32),
            pltpu.VMEM((6, NEV, SITES), BF16),
            pltpu.VMEM((SITES, 2 * EDGE_Y), BF16),
            pltpu.VMEM((6, COLS, SITES), BF16),
        ],
        [SMEM, HBM, HBM, HBM, HBM],
        (
            place,
            pltpu.with_memory_space_constraint(momenta, hbm),
            pltpu.with_memory_space_constraint(vec, hbm),
            pltpu.with_memory_space_constraint(jnp.transpose(gauge_links, (1, 2, 3, 0, 4)), hbm),
            pltpu.with_memory_space_constraint(sol, hbm),
        ),
        "prepare",
        [
            pltpu.SMEM((NMOM, 3), jnp.int32),
            pltpu.VMEM((3, 3, 3, 2, SITES), BF16),
            pltpu.SemaphoreType.DMA((4,)),
        ],
    )
    return [*made[:2], *(in_vmem(a) for a in made[2:])]


def in_vmem(array):
    return pltpu.with_memory_space_constraint(array, pltpu.VMEM)


def body(eigenvectors, gauge_links, solutions, momenta, solution_order):
    vec = eigenvectors.reshape(6, NEV, SITES)
    sol = solutions.reshape(6, COLS, SITES)
    place = jnp.stack((lax.axis_index("gz"), lax.axis_index("gy"))).astype(jnp.int32)
    order = (jnp.tile(solution_order, 4) + (jnp.arange(COLS) // NEV) * NEV).astype(jnp.int32)[None, :]
    y_up, y_down, phase, link, vec, edges, sol = prepare(place, momenta, vec, gauge_links, sol)
    size = lax.axis_size("gy")
    y_up = lax.ppermute(y_up, "gy", [(i, (i - 1) % size) for i in range(size)])
    y_down = lax.ppermute(y_down, "gy", [(i, (i + 1) % size) for i in range(size)])
    slabs = lax.axis_size("gz")

    def across(block, k):
        return lax.ppermute(block, "gz", [(i, (i + k) % slabs) for i in range(slabs)])

    first_two = field_block((None, 0), place, vec, sol, phase, link, ())
    negated = in_vmem(first_two[4])
    from_below, from_above = across(first_two[1], 1), across(first_two[3], 3)
    along_y = field_block(
        (1,), place, vec, sol, phase, link, (y_up, y_down, edges, first_two[2], negated))
    parts = [first_two[0], from_below, from_above]
    parts += [along_y[0], across(along_y[1], 1), across(along_y[2], 2), across(along_y[3], 3)]
    early = in_vmem(call(early_kernel, pltpu.VMEM((3, NEV, 2 * COLS), F32), [VMEM] * 7, parts, "early"))
    along_z = field_block((2,), place, vec, sol, phase, link, (from_above, from_below, negated))
    parts = [along_z[0], across(along_z[1], 1), across(along_z[2], 2), across(along_z[3], 3)]
    shape = jax.ShapeDtypeStruct
    blocks = call(
        middle_kernel,
        [shape((4, 24, 2 * COLS), BF16)] * 4,
        [SMEM] + [VMEM] * 5,
        (place, early, *parts),
        "middle",
        [pltpu.VMEM((16, 24, 2 * COLS), F32)],
    )
    parts = [blocks[0]]
    for m in range(1, 4):
        parts.append(lax.ppermute(blocks[m], "gy", [(i, i ^ m) for i in range(size)]))
    blocks = call(
        second_kernel,
        [shape((24, 2 * COLS), F32)] + [shape((24, 2 * COLS), BF16)] * 3,
        [SMEM] + [VMEM] * 4,
        (place, *parts),
        "second",
    )
    parts = [blocks[0]]
    for d in range(1, 4):
        parts.append(lax.ppermute(blocks[d], "gy", [(i, (i + 4 * d) % size) for i in range(size)]))
    return call(
        last_kernel,
        shape((6, 4, 2, COLS), F32),
        [VMEM] * 5,
        (*parts, order),
        "last",
    )


def solution(mesh):
    return jax.shard_map(
        body,
        mesh=mesh,
        in_specs=(
            P(None, None, None, ("ta", "gz", "gy")),
            P(None, None, None, None, ("ta", "gz", "gy")),
            P(None, None, None, None, ("ta", "gz", "gy")),
            P(),
            P(),
        ),
        out_specs=P(("ta", "gz", "gy"), None, None, None),
        check_vma=False,
    )
```

```python
import functools

import jax
import jax.numpy as jnp
from jax import lax
from jax.experimental import pallas as pl
from jax.experimental.pallas import tpu as pltpu
from jax.sharding import PartitionSpec as P

NEV = 96
COLS = 384
X = 48
LZ = 48
NY = 48
YD = 3
ZD = 8
PLANE = YD * X
SITES = ZD * PLANE
TILE = 128
TILES = SITES // TILE
NMOM = 4
NZ_DEVICES = 4
EDGE_Y = ZD * X
EDGE_Z = 256
ROWS = 6 * NEV
LINK_ROWS = 32
TWO_PI = 6.283185307179586
F32 = jnp.float32
BF16 = jnp.bfloat16
VMEM = pl.BlockSpec(memory_space=pltpu.VMEM)
SMEM = pl.BlockSpec(memory_space=pltpu.SMEM)
HBM = pl.BlockSpec(memory_space=pltpu.HBM)
PARAMS = pltpu.CompilerParams(vmem_limit_bytes=30 * 1024 * 1024)


def dot(a, b, dims):
    return lax.dot_general(a, b, (dims, ((), ())), preferred_element_type=F32)


def row_site(column, row):
    return column + (column // X) * (PLANE - X) + row * X


def selector(row):
    sites = lax.broadcasted_iota(jnp.int32, (SITES, EDGE_Y), 0)
    column = lax.broadcasted_iota(jnp.int32, (1, EDGE_Y), 1)
    return (sites == row_site(column, row)).astype(F32).astype(BF16)


def periodic(product, size):
    wrapped = product - size * jnp.floor(product / size)
    return jnp.where(wrapped >= size, wrapped - size, wrapped)


def wave(turns):
    quarter = jnp.floor(turns * 4.0 + 0.5)
    angle = (turns - quarter * 0.25) * F32(TWO_PI)
    square = angle * angle
    cosine = 1.0 + square * (-0.5 + square * (1 / 24 + square * (-1 / 720 + square * (1 / 40320))))
    sine = angle * (1.0 + square * (-1 / 6 + square * (1 / 120 + square * (-1 / 5040 + square * (1 / 362880)))))
    quadrant = quarter.astype(jnp.int32) & 3
    odd = (quadrant & 1) == 1
    sign_cosine = jnp.where((quadrant == 1) | (quadrant == 2), -1.0, 1.0)
    sign_sine = jnp.where(quadrant >= 2, -1.0, 1.0)
    return jnp.where(odd, sine, cosine) * sign_cosine, jnp.where(odd, cosine, sine) * sign_sine


def prepare_kernel(
    place, momenta_hbm, vec_hbm, link_hbm, sol_hbm,
    y_up, y_down, phase, flat_link, vec, edges, sol,
    momenta, link, sems,
):
    fetches = [
        pltpu.make_async_copy(link_hbm, link, sems.at[0]),
        pltpu.make_async_copy(momenta_hbm, momenta, sems.at[1]),
        pltpu.make_async_copy(vec_hbm, vec, sems.at[2]),
        pltpu.make_async_copy(sol_hbm, sol, sems.at[3]),
    ]
    for fetch in fetches:
        fetch.start()
    edges[:, :EDGE_Y] = selector(0)
    edges[:, EDGE_Y:] = selector(YD - 1)
    fetches[0].wait()
    for q in range(27):
        flat_link[2 * q : 2 * q + 2, :] = link[q // 9, (q // 3) % 3, q % 3].astype(F32)
    pad = jnp.zeros((LINK_ROWS - 18, SITES), F32)
    y_link = jnp.concatenate((flat_link[18:36, :], pad), axis=0).astype(BF16)
    fetches[1].wait()
    sites = lax.broadcasted_iota(jnp.int32, (8, SITES), 1)
    row = lax.broadcasted_iota(jnp.int32, (8, SITES), 0)
    slab = sites // PLANE
    within = sites - slab * PLANE
    line = within // X
    column = (within - line * X).astype(F32)
    slab = (slab + place[0] * ZD).astype(F32)
    line = (line + place[1] * YD).astype(F32)
    along = [jnp.zeros((8, SITES), F32) for _ in range(3)]
    for p in range(NMOM):
        for axis in range(3):
            value = momenta[(place[0] + p) & 3, axis].astype(F32)
            along[axis] = jnp.where((row & 3) == p, value, along[axis])
    x_part = periodic(along[0] * column, float(X)) / X
    y_part = periodic(along[1] * line, float(NY)) / NY
    z_part = periodic(along[2] * slab, float(LZ)) / LZ
    cosine, sine = wave(x_part + y_part + z_part)
    table = jnp.where(row < 4, cosine, sine)
    for k in range(8):
        phase[k] = jnp.broadcast_to(table[k : k + 1, :], (8, SITES))
    fetches[2].wait()
    flat = jnp.concatenate((vec[...].reshape(ROWS, SITES), y_link), axis=0)
    compact = dot(flat, edges[...], ((1,), (0,))).astype(BF16)
    y_up[...] = compact[:ROWS, :EDGE_Y]
    y_down[...] = compact[:, EDGE_Y:]
    fetches[3].wait()


def choose(mask, yes, no):
    parts = (yes.shape[0] // 8, 8, SITES)
    return jnp.where(mask[None], yes.reshape(parts), no.reshape(parts)).reshape(yes.shape)


def shift_x(block, step):
    x = lax.broadcasted_iota(jnp.int32, (8, SITES), 1) % X
    near = pltpu.roll(block, (-step) % SITES, 1)
    far = pltpu.roll(block, (step * (X - 1)) % SITES, 1)
    return choose(x == (X - 1 if step > 0 else 0), far, near)


def shift_y(near, far, step):
    line = (lax.broadcasted_iota(jnp.int32, (8, SITES), 1) // X) % YD
    return choose(line == (YD - 1 if step > 0 else 0), far, near)


def near_kernel(vec, ahead, behind):
    for block in range(6):
        here = vec[block].astype(F32)
        ahead[block] = pltpu.roll(here, SITES - X, 1).astype(BF16)
        behind[block] = pltpu.roll(here, X, 1).astype(BF16)


def shift_z(block, halo, step):
    wide = SITES + EDGE_Z
    if step > 0:
        joined = jnp.concatenate((block, halo), axis=1)
        return pltpu.roll(joined, wide - PLANE, 1)[:, :SITES]
    joined = jnp.concatenate((halo, block), axis=1)
    return pltpu.roll(joined, wide - (EDGE_Z - PLANE), 1)[:, :SITES]


def weigh(field, cosine, sine):
    real, imag = field
    return cosine * real - sine * imag, cosine * imag + sine * real


def rounded(block):
    return block.reshape(16, TILE).astype(BF16).astype(F32).reshape(2, 8, TILE)


def field_tile(direction, vec, ahead, behind, wide, rows, lanes):
    def tile(ref, block):
        return ref[block, rows, lanes].astype(F32).reshape(2, 8, TILE)

    if direction is None:
        return [(tile(vec, c), tile(vec, 3 + c)) for c in range(3)]
    forward = [(tile(ahead, c), tile(ahead, 3 + c)) for c in range(3)]
    back = [(tile(behind, c), tile(behind, 3 + c)) for c in range(3)]
    fields = []
    for a in range(3):
        real = imag = low_real = low_imag = None
        for b in range(3):
            ahead_at, behind_at = 2 * (a * 3 + b), 18 + 2 * (b * 3 + a)
            ur, ui = wide[ahead_at, :, lanes], wide[ahead_at + 1, :, lanes]
            dr, di = wide[behind_at, :, lanes], wide[behind_at + 1, :, lanes]
            vr, vi = forward[b]
            br, bi = back[b]
            terms = (ur * vr - ui * vi, ur * vi + ui * vr, dr * br + di * bi, dr * bi - di * br)
            if b == 0:
                real, imag, low_real, low_imag = terms
            else:
                real, imag, low_real, low_imag = (
                    real + terms[0], imag + terms[1], low_real + terms[2], low_imag + terms[3])
        fields.append((real - rounded(low_real), imag - rounded(low_imag)))
    return fields


def shift_all(direction, place, vec, link, halo, ahead, behind, wide):
    links = link[18 * direction : 18 * direction + 18, :]
    links = jnp.concatenate((links, jnp.zeros((14, SITES), F32)), axis=0)
    if direction == 1:
        above = jnp.concatenate((halo[0][...], jnp.zeros((LINK_ROWS, EDGE_Y), BF16)), axis=0)
        far = dot(jnp.concatenate((halo[1][...], above), axis=1), halo[2][...], ((1,), (1,)))
        ahead[...] = far[:ROWS, :].astype(BF16).reshape(6, NEV, SITES)
    if direction == 2:
        keep_up = (place[0] < NZ_DEVICES - 1).astype(F32)
        keep_down = (place[0] > 0).astype(F32)
    for block in range(6):
        here = vec[block].astype(F32)
        rows = pl.ds(block * NEV, NEV)
        if direction == 0:
            front, rear = shift_x(here, 1), shift_x(here, -1)
        elif direction == 1:
            from_devices = ahead[block].astype(F32)
            front = shift_y(halo[3][block].astype(F32), from_devices, 1)
            rear = shift_y(halo[4][block].astype(F32), from_devices, -1)
        else:
            rows = slice(2 * NEV + block % 2 * NEV, 3 * NEV + block % 2 * NEV)
            columns = slice(block // 2 * EDGE_Z, block // 2 * EDGE_Z + EDGE_Z)
            front = shift_z(here, halo[0][rows, columns].astype(F32) * keep_up, 1)
            rear = shift_z(here, halo[1][rows, columns].astype(F32) * keep_down, -1)
        ahead[block] = front.astype(BF16)
        behind[block] = rear.astype(BF16)
    if direction == 0:
        links_below = shift_x(links, -1)
    elif direction == 1:
        links_below = shift_y(pltpu.roll(links, X, 1), far[ROWS:, :], -1)
    else:
        links_below = shift_z(links, halo[1][4 * NEV :, :EDGE_Z].astype(F32) * keep_down, -1)
    for k in range(18):
        wide[k] = jnp.broadcast_to(links[k : k + 1, :], (8, SITES))
        wide[18 + k] = jnp.broadcast_to(links_below[k : k + 1, :], (8, SITES))


def field_kernel(directions, *refs):
    refs = list(refs)
    place, vec, sol, phase, link = [refs.pop(0) for _ in range(5)]
    halos = [[refs.pop(0) for _ in range(HALOS[d])] for d in directions]
    outs = [refs.pop(0) for _ in range(NMOM)]
    height = NEV * len(directions)
    leads = directions[0] is None
    if leads:
        negated = refs.pop(0)
    else:
        negated = halos[-1].pop()
    if 1 in directions:
        outs[2][NEV:, :] = halos[0].pop()[...]
    weighted = [refs.pop(0), refs.pop(0)]
    total = refs.pop(0)
    shifted = [[refs.pop(0) for _ in range(0 if d is None else 3)] for d in directions]
    for d, halo, kept in zip(directions, halos, shifted):
        if d is not None:
            shift_all(d, place, vec, link, halo, *kept)

    def fill(tile, slot, part):
        lanes = pl.ds(tile * TILE if isinstance(tile, int) else pl.multiple_of(tile * TILE, TILE), TILE)
        for e in range(2 * part, 2 * part + 2):
            for f, d in enumerate(directions):
                ahead, behind, wide = shifted[f] if shifted[f] else (None, None, None)
                fields = field_tile(d, vec, ahead, behind, wide, pl.ds(e * 16, 16), lanes)
                for p in range(NMOM):
                    cosine, sine = phase[p, :, lanes], phase[4 + p, :, lanes]
                    rows = pl.ds((p * len(directions) + f) * NEV + e * 16, 16)
                    for c in range(3):
                        real, imag = weigh(fields[c], cosine, sine)
                        weighted[slot][rows, c * TILE : (c + 1) * TILE] = real.reshape(16, TILE).astype(BF16)
                        weighted[slot][rows, (3 + c) * TILE : (4 + c) * TILE] = imag.reshape(16, TILE).astype(BF16)

    def right_hand(lanes, k, first, stop):
        pieces = []
        if first < COLS:
            pieces.append(sol[k, first : min(stop, COLS), lanes])
        if stop > COLS:
            rows = slice(max(first, COLS) - COLS, stop - COLS)
            pieces.append(sol[3 + k, rows, lanes] if k < 3 else negated[k - 3, rows, lanes])
        return pieces[0] if len(pieces) == 1 else jnp.concatenate(pieces, axis=0)

    def multiply(tile, slot, part):
        lanes = pl.ds(tile * TILE if isinstance(tile, int) else pl.multiple_of(tile * TILE, TILE), TILE)
        columns = pl.ds(part * 256, 256)
        right = jnp.concatenate([right_hand(lanes, k, part * 256, part * 256 + 256) for k in range(6)], axis=1)
        product = dot(weighted[slot][...], right, ((1,), (1,)))
        total[:, columns] = total[:, columns] + product

    for part in range(3):
        fill(0, 0, part)
    if leads:
        for c in range(3):
            negated[c] = -sol[c]
        for third in range(3):
            columns = slice(third * EDGE_Z, third * EDGE_Z + EDGE_Z)
            for b in range(2):
                at = slice(height + b * NEV, height + b * NEV + NEV)
                outs[3][at, columns] = vec[2 * third + b, :, :EDGE_Z]
                outs[1][at, columns] = vec[2 * third + b, :, SITES - EDGE_Z :]
        z_link = jnp.concatenate((link[36:54, SITES - EDGE_Z :], jnp.zeros((LINK_ROWS - 18, EDGE_Z), F32)), axis=0)
        outs[1][height + 2 * NEV :, :EDGE_Z] = z_link.astype(BF16)
        outs[1][height + 2 * NEV :, EDGE_Z:] = jnp.zeros((LINK_ROWS, 2 * EDGE_Z), BF16)
    total[...] = jnp.zeros_like(total)

    def step(i, carry):
        for tile, slot in ((4 * i, 0), (4 * i + 1, 1), (4 * i + 2, 0), (4 * i + 3, 1)):
            for part in range(3):
                multiply(tile, slot, part)
                fill(tile + 1, 1 - slot, part)
        return carry

    lax.fori_loop(0, TILES // 4, step, 0)
    for part in range(3):
        multiply(TILES - 1, 0, part)
    for p in range(NMOM):
        outs[p][:height, :] = total[p * height : (p + 1) * height, :].astype(BF16)


HALOS = {None: 0, 0: 0, 1: 7, 2: 3}


def field_block(directions, place, vec, sol, phase, link, halos):
    height = NEV * len(directions)
    leads = directions[0] is None
    scratch = [
        pltpu.VMEM((NMOM * height, 6 * TILE), BF16),
        pltpu.VMEM((NMOM * height, 6 * TILE), BF16),
        pltpu.VMEM((NMOM * height, 2 * COLS), F32),
    ]
    args = [place, vec, sol, phase, link, *halos]
    specs = [SMEM] + [VMEM] * (len(args) - 1)
    for d in directions:
        if d is not None:
            scratch += [pltpu.VMEM((6, NEV, SITES), BF16)] * 2 + [pltpu.VMEM((36, 8, SITES), F32)]
    tall = [2 * NEV + LINK_ROWS, 0, 2 * NEV] if leads else [0, 2 * NEV if 1 in directions else 0, 0]
    shapes = [jax.ShapeDtypeStruct((height + extra, 2 * COLS), BF16) for extra in (0, *tall)]
    if leads:
        shapes.append(pltpu.VMEM((3, COLS, SITES), BF16))
    return pl.pallas_call(
        functools.partial(field_kernel, directions),
        out_shape=shapes,
        in_specs=specs,
        out_specs=[VMEM] * len(shapes),
        scratch_shapes=scratch,
        compiler_params=PARAMS,
        cost_estimate=pl.CostEstimate(
            flops=8 * len(directions) * 384 * 768 * 6912, bytes_accessed=6_000_000, transcendentals=0),
        name="field_block",
    )(*args)


def total_of(terms):
    summed = terms[0].astype(F32)
    for term in terms[1:]:
        summed = summed + term.astype(F32)
    return summed


def early_kernel(*refs):
    lead, y, out = refs[:3], refs[3:7], refs[7]
    for g in range(2):
        rows = slice(g * NEV, g * NEV + NEV)
        out[g] = total_of([ref[rows, :] for ref in lead] + [y[2][NEV + g * NEV : 2 * NEV + g * NEV, :]])
    out[2] = total_of([ref[:NEV, :] for ref in y])


def middle_kernel(place, early, *refs):
    outs, held = refs[4:8], refs[8]
    for g in range(4):
        summed = early[g] if g < 3 else total_of([ref[...] for ref in refs[:4]])
        for owner in range(16):
            held[owner, g * 6 : g * 6 + 6, :] = summed[owner * 6 : owner * 6 + 6, :]
    low = place[1] & 3
    for m in range(4):
        for q in range(4):
            outs[m][q] = held[q * 4 + (low ^ m)].astype(BF16)


def second_kernel(place, own, one, two, three, *outs):
    high = place[1] // 4
    for d in range(4):
        at = (high + d) & 3
        summed = own[at].astype(F32)
        for ref in (one, two, three):
            summed = summed + ref[at].astype(F32)
        outs[d][...] = summed.astype(outs[d].dtype)


def last_kernel(own, one, two, three, order, out):
    below = lax.broadcasted_iota(jnp.int32, (COLS, COLS), 0)
    moves = (below == order[...]).astype(F32).astype(BF16)
    summed = own[...]
    for ref in (one, two, three):
        summed = summed + ref[...].astype(F32)
    for r in range(2):
        rest = summed[:, r * COLS : (r + 1) * COLS]
        moved = None
        for _ in range(3):
            part = rest.astype(BF16)
            rest = rest - part.astype(F32)
            term = dot(part, moves, ((1,), (0,)))
            moved = term if moved is None else moved + term
        for g in range(4):
            out[:, g, r, :] = moved[g * 6 : g * 6 + 6, :]


def call(kernel, shapes, specs, args, name, scratch=()):
    many = isinstance(shapes, list)
    return pl.pallas_call(
        kernel,
        out_shape=shapes,
        in_specs=specs,
        out_specs=[VMEM] * len(shapes) if many else VMEM,
        scratch_shapes=list(scratch),
        compiler_params=PARAMS,
        name=name,
    )(*args)


def prepare(place, momenta, vec, gauge_links, sol):
    shape = jax.ShapeDtypeStruct
    hbm = pltpu.MemorySpace.HBM
    made = call(
        prepare_kernel,
        [
            shape((ROWS, EDGE_Y), BF16),
            shape((ROWS + LINK_ROWS, EDGE_Y), BF16),
            pltpu.VMEM((8, 8, SITES), F32),
            pltpu.VMEM((54, SITES), F32),
            pltpu.VMEM((6, NEV, SITES), BF16),
            pltpu.VMEM((SITES, 2 * EDGE_Y), BF16),
            pltpu.VMEM((6, COLS, SITES), BF16),
        ],
        [SMEM, HBM, HBM, HBM, HBM],
        (
            place,
            pltpu.with_memory_space_constraint(momenta, hbm),
            pltpu.with_memory_space_constraint(vec, hbm),
            pltpu.with_memory_space_constraint(jnp.transpose(gauge_links, (1, 2, 3, 0, 4)), hbm),
            pltpu.with_memory_space_constraint(sol, hbm),
        ),
        "prepare",
        [
            pltpu.SMEM((NMOM, 3), jnp.int32),
            pltpu.VMEM((3, 3, 3, 2, SITES), BF16),
            pltpu.SemaphoreType.DMA((4,)),
        ],
    )
    return [*made[:2], *(in_vmem(a) for a in made[2:])]


def in_vmem(array):
    return pltpu.with_memory_space_constraint(array, pltpu.VMEM)


def body(eigenvectors, gauge_links, solutions, momenta, solution_order):
    vec = eigenvectors.reshape(6, NEV, SITES)
    sol = solutions.reshape(6, COLS, SITES)
    place = jnp.stack((lax.axis_index("gz"), lax.axis_index("gy"))).astype(jnp.int32)
    order = (jnp.tile(solution_order, 4) + (jnp.arange(COLS) // NEV) * NEV).astype(jnp.int32)[None, :]
    y_up, y_down, phase, link, vec, edges, sol = prepare(place, momenta, vec, gauge_links, sol)
    size = lax.axis_size("gy")
    y_up = lax.ppermute(y_up, "gy", [(i, (i - 1) % size) for i in range(size)])
    y_down = lax.ppermute(y_down, "gy", [(i, (i + 1) % size) for i in range(size)])
    slabs = lax.axis_size("gz")

    def across(block, k):
        return lax.ppermute(block, "gz", [(i, (i + k) % slabs) for i in range(slabs)])

    first_two = field_block((None, 0), place, vec, sol, phase, link, ())
    negated = in_vmem(first_two[4])
    from_below, from_above = across(first_two[1], 1), across(first_two[3], 3)
    near = call(near_kernel, [pltpu.VMEM((6, NEV, SITES), BF16)] * 2, [VMEM], (vec,), "near")
    near = [in_vmem(block) for block in near]
    along_y = field_block(
        (1,), place, vec, sol, phase, link, (y_up, y_down, edges, *near, first_two[2], negated))
    parts = [first_two[0], from_below, from_above]
    parts += [along_y[0], across(along_y[1], 1), across(along_y[2], 2), across(along_y[3], 3)]
    early = in_vmem(call(early_kernel, pltpu.VMEM((3, NEV, 2 * COLS), F32), [VMEM] * 7, parts, "early"))
    along_z = field_block((2,), place, vec, sol, phase, link, (from_above, from_below, negated))
    parts = [along_z[0], across(along_z[1], 1), across(along_z[2], 2), across(along_z[3], 3)]
    shape = jax.ShapeDtypeStruct
    blocks = call(
        middle_kernel,
        [shape((4, 24, 2 * COLS), BF16)] * 4,
        [SMEM] + [VMEM] * 5,
        (place, early, *parts),
        "middle",
        [pltpu.VMEM((16, 24, 2 * COLS), F32)],
    )
    parts = [blocks[0]]
    for m in range(1, 4):
        parts.append(lax.ppermute(blocks[m], "gy", [(i, i ^ m) for i in range(size)]))
    blocks = call(
        second_kernel,
        [shape((24, 2 * COLS), F32)] + [shape((24, 2 * COLS), BF16)] * 3,
        [SMEM] + [VMEM] * 4,
        (place, *parts),
        "second",
    )
    parts = [blocks[0]]
    for d in range(1, 4):
        parts.append(lax.ppermute(blocks[d], "gy", [(i, (i + 4 * d) % size) for i in range(size)]))
    return call(
        last_kernel,
        shape((6, 4, 2, COLS), F32),
        [VMEM] * 5,
        (*parts, order),
        "last",
    )


def solution(mesh):
    return jax.shard_map(
        body,
        mesh=mesh,
        in_specs=(
            P(None, None, None, ("ta", "gz", "gy")),
            P(None, None, None, None, ("ta", "gz", "gy")),
            P(None, None, None, None, ("ta", "gz", "gy")),
            P(),
            P(),
        ),
        out_specs=P(("ta", "gz", "gy"), None, None, None),
        check_vma=False,
    )
```

```python
import functools

import jax
import jax.numpy as jnp
from jax import lax
from jax.experimental import pallas as pl
from jax.experimental.pallas import tpu as pltpu
from jax.sharding import PartitionSpec as P

NEV = 96
COLS = 384
X = 48
LZ = 48
NY = 48
YD = 3
ZD = 8
PLANE = YD * X
SITES = ZD * PLANE
TILE = 128
TILES = SITES // TILE
NMOM = 4
NZ_DEVICES = 4
EDGE_Y = ZD * X
EDGE_Z = 256
ROWS = 6 * NEV
LINK_ROWS = 32
TWO_PI = 6.283185307179586
F32 = jnp.float32
BF16 = jnp.bfloat16
VMEM = pl.BlockSpec(memory_space=pltpu.VMEM)
SMEM = pl.BlockSpec(memory_space=pltpu.SMEM)
HBM = pl.BlockSpec(memory_space=pltpu.HBM)
PARAMS = pltpu.CompilerParams(vmem_limit_bytes=30 * 1024 * 1024)


def dot(a, b, dims):
    return lax.dot_general(a, b, (dims, ((), ())), preferred_element_type=F32)


def row_site(column, row):
    return column + (column // X) * (PLANE - X) + row * X


def selector(row):
    sites = lax.broadcasted_iota(jnp.int32, (SITES, EDGE_Y), 0)
    column = lax.broadcasted_iota(jnp.int32, (1, EDGE_Y), 1)
    return (sites == row_site(column, row)).astype(F32).astype(BF16)


def periodic(product, size):
    wrapped = product - size * jnp.floor(product / size)
    return jnp.where(wrapped >= size, wrapped - size, wrapped)


def wave(turns):
    quarter = jnp.floor(turns * 4.0 + 0.5)
    angle = (turns - quarter * 0.25) * F32(TWO_PI)
    square = angle * angle
    cosine = 1.0 + square * (-0.5 + square * (1 / 24 + square * (-1 / 720 + square * (1 / 40320))))
    sine = angle * (1.0 + square * (-1 / 6 + square * (1 / 120 + square * (-1 / 5040 + square * (1 / 362880)))))
    quadrant = quarter.astype(jnp.int32) & 3
    odd = (quadrant & 1) == 1
    sign_cosine = jnp.where((quadrant == 1) | (quadrant == 2), -1.0, 1.0)
    sign_sine = jnp.where(quadrant >= 2, -1.0, 1.0)
    return jnp.where(odd, sine, cosine) * sign_cosine, jnp.where(odd, cosine, sine) * sign_sine


def prepare_kernel(
    place, momenta_hbm, vec_hbm, link_hbm, sol_hbm,
    y_up, y_down, phase, flat_link, vec, edges, sol,
    momenta, link, sems,
):
    fetches = [
        pltpu.make_async_copy(link_hbm, link, sems.at[0]),
        pltpu.make_async_copy(momenta_hbm, momenta, sems.at[1]),
        pltpu.make_async_copy(vec_hbm, vec, sems.at[2]),
        pltpu.make_async_copy(sol_hbm, sol, sems.at[3]),
    ]
    for fetch in fetches:
        fetch.start()
    edges[:, :EDGE_Y] = selector(0)
    edges[:, EDGE_Y:] = selector(YD - 1)
    fetches[0].wait()
    for q in range(27):
        flat_link[2 * q : 2 * q + 2, :] = link[q // 9, (q // 3) % 3, q % 3].astype(F32)
    pad = jnp.zeros((LINK_ROWS - 18, SITES), F32)
    y_link = jnp.concatenate((flat_link[18:36, :], pad), axis=0).astype(BF16)
    fetches[1].wait()
    sites = lax.broadcasted_iota(jnp.int32, (8, SITES), 1)
    row = lax.broadcasted_iota(jnp.int32, (8, SITES), 0)
    slab = sites // PLANE
    within = sites - slab * PLANE
    line = within // X
    column = (within - line * X).astype(F32)
    slab = (slab + place[0] * ZD).astype(F32)
    line = (line + place[1] * YD).astype(F32)
    along = [jnp.zeros((8, SITES), F32) for _ in range(3)]
    for p in range(NMOM):
        for axis in range(3):
            value = momenta[(place[0] + p) & 3, axis].astype(F32)
            along[axis] = jnp.where((row & 3) == p, value, along[axis])
    x_part = periodic(along[0] * column, float(X)) / X
    y_part = periodic(along[1] * line, float(NY)) / NY
    z_part = periodic(along[2] * slab, float(LZ)) / LZ
    cosine, sine = wave(x_part + y_part + z_part)
    table = jnp.where(row < 4, cosine, sine)
    for k in range(8):
        phase[k] = jnp.broadcast_to(table[k : k + 1, :], (8, SITES))
    fetches[2].wait()
    flat = jnp.concatenate((vec[...].reshape(ROWS, SITES), y_link), axis=0)
    compact = dot(flat, edges[...], ((1,), (0,))).astype(BF16)
    y_up[...] = compact[:ROWS, :EDGE_Y]
    y_down[...] = compact[:, EDGE_Y:]
    fetches[3].wait()


def choose(mask, yes, no):
    parts = (yes.shape[0] // 8, 8, SITES)
    return jnp.where(mask[None], yes.reshape(parts), no.reshape(parts)).reshape(yes.shape)


def shift_x(block, step):
    x = lax.broadcasted_iota(jnp.int32, (8, SITES), 1) % X
    near = pltpu.roll(block, (-step) % SITES, 1)
    far = pltpu.roll(block, (step * (X - 1)) % SITES, 1)
    return choose(x == (X - 1 if step > 0 else 0), far, near)


def shift_y(near, far, step):
    line = (lax.broadcasted_iota(jnp.int32, (8, SITES), 1) // X) % YD
    return choose(line == (YD - 1 if step > 0 else 0), far, near)


def near_kernel(vec, ahead, behind, above, below):
    for block in range(6):
        here = vec[block].astype(F32)
        ahead[block] = pltpu.roll(here, SITES - X, 1).astype(BF16)
        behind[block] = pltpu.roll(here, X, 1).astype(BF16)
        above[block] = pltpu.roll(here, SITES - PLANE, 1).astype(BF16)
        below[block] = pltpu.roll(here, PLANE, 1).astype(BF16)


def shift_z(block, halo, step):
    wide = SITES + EDGE_Z
    if step > 0:
        joined = jnp.concatenate((block, halo), axis=1)
        return pltpu.roll(joined, wide - PLANE, 1)[:, :SITES]
    joined = jnp.concatenate((halo, block), axis=1)
    return pltpu.roll(joined, wide - (EDGE_Z - PLANE), 1)[:, :SITES]


def weigh(field, cosine, sine):
    real, imag = field
    return cosine * real - sine * imag, cosine * imag + sine * real


def rounded(block):
    return block.reshape(16, TILE).astype(BF16).astype(F32).reshape(2, 8, TILE)


def field_tile(direction, vec, ahead, behind, wide, rows, lanes):
    def tile(ref, block):
        return ref[block, rows, lanes].astype(F32).reshape(2, 8, TILE)

    if direction is None:
        return [(tile(vec, c), tile(vec, 3 + c)) for c in range(3)]
    forward = [(tile(ahead, c), tile(ahead, 3 + c)) for c in range(3)]
    back = [(tile(behind, c), tile(behind, 3 + c)) for c in range(3)]
    fields = []
    for a in range(3):
        real = imag = low_real = low_imag = None
        for b in range(3):
            ahead_at, behind_at = 2 * (a * 3 + b), 18 + 2 * (b * 3 + a)
            ur, ui = wide[ahead_at, :, lanes], wide[ahead_at + 1, :, lanes]
            dr, di = wide[behind_at, :, lanes], wide[behind_at + 1, :, lanes]
            vr, vi = forward[b]
            br, bi = back[b]
            terms = (ur * vr - ui * vi, ur * vi + ui * vr, dr * br + di * bi, dr * bi - di * br)
            if b == 0:
                real, imag, low_real, low_imag = terms
            else:
                real, imag, low_real, low_imag = (
                    real + terms[0], imag + terms[1], low_real + terms[2], low_imag + terms[3])
        fields.append((real - rounded(low_real), imag - rounded(low_imag)))
    return fields


def shift_all(direction, place, vec, link, halo, ahead, behind, wide):
    links = link[18 * direction : 18 * direction + 18, :]
    links = jnp.concatenate((links, jnp.zeros((14, SITES), F32)), axis=0)
    if direction == 1:
        above = jnp.concatenate((halo[0][...], jnp.zeros((LINK_ROWS, EDGE_Y), BF16)), axis=0)
        far = dot(jnp.concatenate((halo[1][...], above), axis=1), halo[2][...], ((1,), (1,)))
        ahead[...] = far[:ROWS, :].astype(BF16).reshape(6, NEV, SITES)
    if direction == 2:
        keep_up = (place[0] < NZ_DEVICES - 1).astype(F32)
        keep_down = (place[0] > 0).astype(F32)
    for block in range(6):
        here = vec[block].astype(F32)
        rows = pl.ds(block * NEV, NEV)
        if direction == 0:
            front, rear = shift_x(here, 1), shift_x(here, -1)
        elif direction == 1:
            from_devices = ahead[block].astype(F32)
            front = shift_y(halo[3][block].astype(F32), from_devices, 1)
            rear = shift_y(halo[4][block].astype(F32), from_devices, -1)
        else:
            rows = slice(2 * NEV + block % 2 * NEV, 3 * NEV + block % 2 * NEV)
            columns = slice(block // 2 * EDGE_Z, block // 2 * EDGE_Z + EDGE_Z)
            lane = lax.broadcasted_iota(jnp.int32, (NEV, EDGE_Z), 1)
            up = pltpu.roll(halo[0][rows, columns].astype(F32) * keep_up, EDGE_Z - PLANE, 1)
            down = pltpu.roll(halo[1][rows, columns].astype(F32) * keep_down, PLANE, 1)
            front, rear = halo[2][block].astype(F32), halo[3][block].astype(F32)
            top = jnp.where(lane >= EDGE_Z - PLANE, up, front[:, SITES - EDGE_Z :])
            bottom = jnp.where(lane < PLANE, down, rear[:, :EDGE_Z])
            front = jnp.concatenate((front[:, : SITES - EDGE_Z], top), axis=1)
            rear = jnp.concatenate((bottom, rear[:, EDGE_Z:]), axis=1)
        ahead[block] = front.astype(BF16)
        behind[block] = rear.astype(BF16)
    if direction == 0:
        links_below = shift_x(links, -1)
    elif direction == 1:
        links_below = shift_y(pltpu.roll(links, X, 1), far[ROWS:, :], -1)
    else:
        links_below = shift_z(links, halo[1][4 * NEV :, :EDGE_Z].astype(F32) * keep_down, -1)
    for k in range(18):
        wide[k] = jnp.broadcast_to(links[k : k + 1, :], (8, SITES))
        wide[18 + k] = jnp.broadcast_to(links_below[k : k + 1, :], (8, SITES))


def field_kernel(directions, *refs):
    refs = list(refs)
    place, vec, sol, phase, link = [refs.pop(0) for _ in range(5)]
    halos = [[refs.pop(0) for _ in range(HALOS[d])] for d in directions]
    outs = [refs.pop(0) for _ in range(NMOM)]
    height = NEV * len(directions)
    leads = directions[0] is None
    if leads:
        negated = refs.pop(0)
    else:
        negated = halos[-1].pop()
    if 1 in directions:
        outs[2][NEV:, :] = halos[0].pop()[...]
    weighted = [refs.pop(0), refs.pop(0)]
    total = refs.pop(0)
    shifted = [[refs.pop(0) for _ in range(0 if d is None else 3)] for d in directions]
    for d, halo, kept in zip(directions, halos, shifted):
        if d is not None:
            shift_all(d, place, vec, link, halo, *kept)

    def fill(tile, slot, part):
        lanes = pl.ds(tile * TILE if isinstance(tile, int) else pl.multiple_of(tile * TILE, TILE), TILE)
        for e in range(2 * part, 2 * part + 2):
            for f, d in enumerate(directions):
                ahead, behind, wide = shifted[f] if shifted[f] else (None, None, None)
                fields = field_tile(d, vec, ahead, behind, wide, pl.ds(e * 16, 16), lanes)
                for p in range(NMOM):
                    cosine, sine = phase[p, :, lanes], phase[4 + p, :, lanes]
                    rows = pl.ds((p * len(directions) + f) * NEV + e * 16, 16)
                    for c in range(3):
                        real, imag = weigh(fields[c], cosine, sine)
                        weighted[slot][rows, c * TILE : (c + 1) * TILE] = real.reshape(16, TILE).astype(BF16)
                        weighted[slot][rows, (3 + c) * TILE : (4 + c) * TILE] = imag.reshape(16, TILE).astype(BF16)

    def right_hand(lanes, k, first, stop):
        pieces = []
        if first < COLS:
            pieces.append(sol[k, first : min(stop, COLS), lanes])
        if stop > COLS:
            rows = slice(max(first, COLS) - COLS, stop - COLS)
            pieces.append(sol[3 + k, rows, lanes] if k < 3 else negated[k - 3, rows, lanes])
        return pieces[0] if len(pieces) == 1 else jnp.concatenate(pieces, axis=0)

    def multiply(tile, slot, part):
        lanes = pl.ds(tile * TILE if isinstance(tile, int) else pl.multiple_of(tile * TILE, TILE), TILE)
        columns = pl.ds(part * 256, 256)
        right = jnp.concatenate([right_hand(lanes, k, part * 256, part * 256 + 256) for k in range(6)], axis=1)
        product = dot(weighted[slot][...], right, ((1,), (1,)))
        total[:, columns] = total[:, columns] + product

    for part in range(3):
        fill(0, 0, part)
    if leads:
        for c in range(3):
            negated[c] = -sol[c]
        for third in range(3):
            columns = slice(third * EDGE_Z, third * EDGE_Z + EDGE_Z)
            for b in range(2):
                at = slice(height + b * NEV, height + b * NEV + NEV)
                outs[3][at, columns] = vec[2 * third + b, :, :EDGE_Z]
                outs[1][at, columns] = vec[2 * third + b, :, SITES - EDGE_Z :]
        z_link = jnp.concatenate((link[36:54, SITES - EDGE_Z :], jnp.zeros((LINK_ROWS - 18, EDGE_Z), F32)), axis=0)
        outs[1][height + 2 * NEV :, :EDGE_Z] = z_link.astype(BF16)
        outs[1][height + 2 * NEV :, EDGE_Z:] = jnp.zeros((LINK_ROWS, 2 * EDGE_Z), BF16)
    total[...] = jnp.zeros_like(total)

    def step(i, carry):
        for tile, slot in ((4 * i, 0), (4 * i + 1, 1), (4 * i + 2, 0), (4 * i + 3, 1)):
            for part in range(3):
                multiply(tile, slot, part)
                fill(tile + 1, 1 - slot, part)
        return carry

    lax.fori_loop(0, TILES // 4, step, 0)
    for part in range(3):
        multiply(TILES - 1, 0, part)
    for p in range(NMOM):
        outs[p][:height, :] = total[p * height : (p + 1) * height, :].astype(BF16)


HALOS = {None: 0, 0: 0, 1: 7, 2: 5}


def field_block(directions, place, vec, sol, phase, link, halos):
    height = NEV * len(directions)
    leads = directions[0] is None
    scratch = [
        pltpu.VMEM((NMOM * height, 6 * TILE), BF16),
        pltpu.VMEM((NMOM * height, 6 * TILE), BF16),
        pltpu.VMEM((NMOM * height, 2 * COLS), F32),
    ]
    args = [place, vec, sol, phase, link, *halos]
    specs = [SMEM] + [VMEM] * (len(args) - 1)
    for d in directions:
        if d is not None:
            scratch += [pltpu.VMEM((6, NEV, SITES), BF16)] * 2 + [pltpu.VMEM((36, 8, SITES), F32)]
    tall = [2 * NEV + LINK_ROWS, 0, 2 * NEV] if leads else [0, 2 * NEV if 1 in directions else 0, 0]
    shapes = [jax.ShapeDtypeStruct((height + extra, 2 * COLS), BF16) for extra in (0, *tall)]
    if leads:
        shapes.append(pltpu.VMEM((3, COLS, SITES), BF16))
    return pl.pallas_call(
        functools.partial(field_kernel, directions),
        out_shape=shapes,
        in_specs=specs,
        out_specs=[VMEM] * len(shapes),
        scratch_shapes=scratch,
        compiler_params=PARAMS,
        cost_estimate=pl.CostEstimate(
            flops=8 * len(directions) * 384 * 768 * 6912, bytes_accessed=6_000_000, transcendentals=0),
        name="field_block",
    )(*args)


def total_of(terms):
    summed = terms[0].astype(F32)
    for term in terms[1:]:
        summed = summed + term.astype(F32)
    return summed


def early_kernel(*refs):
    lead, y, out = refs[:3], refs[3:7], refs[7]
    for g in range(2):
        rows = slice(g * NEV, g * NEV + NEV)
        out[g] = total_of([ref[rows, :] for ref in lead] + [y[2][NEV + g * NEV : 2 * NEV + g * NEV, :]])
    out[2] = total_of([ref[:NEV, :] for ref in y])


def middle_kernel(place, early, *refs):
    outs, held = refs[4:8], refs[8]
    for g in range(4):
        summed = early[g] if g < 3 else total_of([ref[...] for ref in refs[:4]])
        for owner in range(16):
            held[owner, g * 6 : g * 6 + 6, :] = summed[owner * 6 : owner * 6 + 6, :]
    low = place[1] & 3
    for m in range(4):
        for q in range(4):
            outs[m][q] = held[q * 4 + (low ^ m)].astype(BF16)


def second_kernel(place, own, one, two, three, *outs):
    high = place[1] // 4
    for d in range(4):
        at = (high + d) & 3
        summed = own[at].astype(F32)
        for ref in (one, two, three):
            summed = summed + ref[at].astype(F32)
        outs[d][...] = summed.astype(outs[d].dtype)


def last_kernel(own, one, two, three, order, out):
    below = lax.broadcasted_iota(jnp.int32, (COLS, COLS), 0)
    moves = (below == order[...]).astype(F32).astype(BF16)
    summed = own[...]
    for ref in (one, two, three):
        summed = summed + ref[...].astype(F32)
    for r in range(2):
        rest = summed[:, r * COLS : (r + 1) * COLS]
        moved = None
        for _ in range(3):
            part = rest.astype(BF16)
            rest = rest - part.astype(F32)
            term = dot(part, moves, ((1,), (0,)))
            moved = term if moved is None else moved + term
        for g in range(4):
            out[:, g, r, :] = moved[g * 6 : g * 6 + 6, :]


def call(kernel, shapes, specs, args, name, scratch=()):
    many = isinstance(shapes, list)
    return pl.pallas_call(
        kernel,
        out_shape=shapes,
        in_specs=specs,
        out_specs=[VMEM] * len(shapes) if many else VMEM,
        scratch_shapes=list(scratch),
        compiler_params=PARAMS,
        name=name,
    )(*args)


def prepare(place, momenta, vec, gauge_links, sol):
    shape = jax.ShapeDtypeStruct
    hbm = pltpu.MemorySpace.HBM
    made = call(
        prepare_kernel,
        [
            shape((ROWS, EDGE_Y), BF16),
            shape((ROWS + LINK_ROWS, EDGE_Y), BF16),
            pltpu.VMEM((8, 8, SITES), F32),
            pltpu.VMEM((54, SITES), F32),
            pltpu.VMEM((6, NEV, SITES), BF16),
            pltpu.VMEM((SITES, 2 * EDGE_Y), BF16),
            pltpu.VMEM((6, COLS, SITES), BF16),
        ],
        [SMEM, HBM, HBM, HBM, HBM],
        (
            place,
            pltpu.with_memory_space_constraint(momenta, hbm),
            pltpu.with_memory_space_constraint(vec, hbm),
            pltpu.with_memory_space_constraint(jnp.transpose(gauge_links, (1, 2, 3, 0, 4)), hbm),
            pltpu.with_memory_space_constraint(sol, hbm),
        ),
        "prepare",
        [
            pltpu.SMEM((NMOM, 3), jnp.int32),
            pltpu.VMEM((3, 3, 3, 2, SITES), BF16),
            pltpu.SemaphoreType.DMA((4,)),
        ],
    )
    return [*made[:2], *(in_vmem(a) for a in made[2:])]


def in_vmem(array):
    return pltpu.with_memory_space_constraint(array, pltpu.VMEM)


def body(eigenvectors, gauge_links, solutions, momenta, solution_order):
    vec = eigenvectors.reshape(6, NEV, SITES)
    sol = solutions.reshape(6, COLS, SITES)
    place = jnp.stack((lax.axis_index("gz"), lax.axis_index("gy"))).astype(jnp.int32)
    order = (jnp.tile(solution_order, 4) + (jnp.arange(COLS) // NEV) * NEV).astype(jnp.int32)[None, :]
    y_up, y_down, phase, link, vec, edges, sol = prepare(place, momenta, vec, gauge_links, sol)
    size = lax.axis_size("gy")
    y_up = lax.ppermute(y_up, "gy", [(i, (i - 1) % size) for i in range(size)])
    y_down = lax.ppermute(y_down, "gy", [(i, (i + 1) % size) for i in range(size)])
    slabs = lax.axis_size("gz")

    def across(block, k):
        return lax.ppermute(block, "gz", [(i, (i + k) % slabs) for i in range(slabs)])

    first_two = field_block((None, 0), place, vec, sol, phase, link, ())
    negated = in_vmem(first_two[4])
    from_below, from_above = across(first_two[1], 1), across(first_two[3], 3)
    near = call(near_kernel, [pltpu.VMEM((6, NEV, SITES), BF16)] * 4, [VMEM], (vec,), "near")
    near = [in_vmem(block) for block in near]
    along_y = field_block(
        (1,), place, vec, sol, phase, link, (y_up, y_down, edges, *near[:2], first_two[2], negated))
    parts = [first_two[0], from_below, from_above]
    parts += [along_y[0], across(along_y[1], 1), across(along_y[2], 2), across(along_y[3], 3)]
    early = in_vmem(call(early_kernel, pltpu.VMEM((3, NEV, 2 * COLS), F32), [VMEM] * 7, parts, "early"))
    along_z = field_block((2,), place, vec, sol, phase, link, (from_above, from_below, *near[2:], negated))
    parts = [along_z[0], across(along_z[1], 1), across(along_z[2], 2), across(along_z[3], 3)]
    shape = jax.ShapeDtypeStruct
    blocks = call(
        middle_kernel,
        [shape((4, 24, 2 * COLS), BF16)] * 4,
        [SMEM] + [VMEM] * 5,
        (place, early, *parts),
        "middle",
        [pltpu.VMEM((16, 24, 2 * COLS), F32)],
    )
    parts = [blocks[0]]
    for m in range(1, 4):
        parts.append(lax.ppermute(blocks[m], "gy", [(i, i ^ m) for i in range(size)]))
    blocks = call(
        second_kernel,
        [shape((24, 2 * COLS), F32)] + [shape((24, 2 * COLS), BF16)] * 3,
        [SMEM] + [VMEM] * 4,
        (place, *parts),
        "second",
    )
    parts = [blocks[0]]
    for d in range(1, 4):
        parts.append(lax.ppermute(blocks[d], "gy", [(i, (i + 4 * d) % size) for i in range(size)]))
    return call(
        last_kernel,
        shape((6, 4, 2, COLS), F32),
        [VMEM] * 5,
        (*parts, order),
        "last",
    )


def solution(mesh):
    return jax.shard_map(
        body,
        mesh=mesh,
        in_specs=(
            P(None, None, None, ("ta", "gz", "gy")),
            P(None, None, None, None, ("ta", "gz", "gy")),
            P(None, None, None, None, ("ta", "gz", "gy")),
            P(),
            P(),
        ),
        out_specs=P(("ta", "gz", "gy"), None, None, None),
        check_vma=False,
    )
```
